256 devices in a mesh: slab: 64 (over y_hi, z, x), col: 4 (over y_lo, core).
Axes of the slice: x: 4, y: 4 (y_hi: 2, y_lo: 2; y = y_hi * 2 + y_lo), z: 8, core: 2. Of those that a mesh axis runs over, the one named last changes fastest.
Arguments:
- start: float32 [131072, 512], P('slab', 'col'), may hold values from -6 to 6
- blocks: float32 [1024, 8, 128, 128], P('slab'), may hold values from -0.1875 to 0.1875
- neighbors: int32 [1024, 8], P('slab'), may hold values from 0 to 15
- offsets: int32 [1024, 8], P('slab'), may hold values from -2 to 2
- center: float32 [1], replicated, may hold values from -0.3 to 0.3
- half_width: float32 [1], replicated, may hold values from 1.5 to 2.5
Outputs:
- filtered: float32 [131072, 512], P('slab', 'col')
- gram: float32 [512, 512], P('col')
- projected: float32 [512, 512], P('col')
The draws below stay inside these ranges and needn't reach their ends.
All inputs are finite; a program needn't handle non-finite values.
Results may differ from the reference program's by a relative error of at most 0.0003.
Values sent between devices are 32-bit elements; how exact they have to be, the bound alone decides.
No kernel may reach another device: no remote copies, remote signals or barrier semaphores. Data moves between devices by JAX's collectives and lax.ppermute only.
A program may use at most 128 MiB of HBM per device.

```python
import jax
import jax.numpy as jnp
from jax import lax

BLOCK = 128
NVEC = 512
NB = 8
FILTER = 3
BLK_DEV = 16
BLK_TOTAL = 1024
ORBITALS = 131072
N_SLAB = 64


def set_ends(entries, key, smallest, largest):
    place = [jax.random.randint(jax.random.fold_in(key, axis), (), 0, length) for axis, length in enumerate(entries.shape)]
    main_axis = entries.shape.index(max(entries.shape))
    beside = place[:main_axis] + [(place[main_axis] + 1) % entries.shape[main_axis]] + place[main_axis + 1:]
    return entries.at[tuple(place)].set(smallest).at[tuple(beside)].set(largest)


def steps_of(own_key, dims, pieces, low, top_value):
    def one(dim, shards_of):
        draws = jax.random.uniform(jax.random.fold_in(jax.random.fold_in(own_key, 6), dim), (shards_of,), jnp.float32, low / len(pieces), top_value / len(pieces))
        return jnp.repeat(jnp.exp(draws), dims[dim] // shards_of).reshape((-1,) + (1,) * (len(dims) - dim - 1))

    gain = one(*pieces[0])
    for cut in pieces[1:]:
        gain = gain * one(*cut)
    return gain


def gaussian(key, shape, spread, most, shards=(), kind=jnp.bfloat16):
    values = jax.random.normal(key, shape, jnp.float32) * spread
    if len(shards) > 0:
        values = steps_of(key, shape, shards, -0.22, 0.18) * values
    return jnp.clip(values, min=-most, max=most).astype(kind)


def setup_inputs(seed: int = 0) -> dict:
    seeds = jax.random.split(jax.random.key(seed), 7)
    return {
        "start": gaussian(seeds[0], (ORBITALS, NVEC), 1.0, 6.0, ((0, 64), (1, 4)), jnp.float32),
        "blocks": gaussian(seeds[1], (BLK_TOTAL, NB, BLOCK, BLOCK), (NB * BLOCK) ** -0.5, 0.1875, ((0, 64),), jnp.float32),
        "neighbors": set_ends(jax.random.randint(seeds[2], (BLK_TOTAL, NB), 0, BLK_DEV), jax.random.fold_in(seeds[2], 1), 0, BLK_DEV - 1).astype(jnp.int32),
        "offsets": set_ends(jax.random.randint(seeds[3], (BLK_TOTAL, NB), -2, 3), jax.random.fold_in(seeds[3], 1), -2, 2).astype(jnp.int32),
        "center": jnp.clip(jax.random.uniform(seeds[4], (1,), jnp.float32, -0.3, 0.3), -0.3, 0.3),
        "half_width": jnp.clip(jax.random.uniform(seeds[5], (1,), jnp.float32, 1.5, 2.5), 1.5, 2.5),
    }


def apply_operator(vectors, blocks, neighbors, offsets):
    grid = vectors.reshape(BLK_DEV * N_SLAB, BLOCK, NVEC)
    slab_ids = jnp.arange(N_SLAB, dtype=jnp.int32)

    def one_slab(items):
        slab_blocks, slab_nbrs, slab_offs, slab_id = items
        source = ((slab_id + slab_offs) % N_SLAB) * BLK_DEV + slab_nbrs
        taken = grid[source.astype(jnp.int32)]
        return jnp.einsum("inab,inbc->iac", slab_blocks, taken, precision=lax.Precision.HIGHEST)

    result = lax.map(one_slab, (blocks.reshape(N_SLAB, BLK_DEV, NB, BLOCK, BLOCK),
                                neighbors.reshape(N_SLAB, BLK_DEV, NB),
                                offsets.reshape(N_SLAB, BLK_DEV, NB), slab_ids))
    return result.reshape(BLK_DEV * N_SLAB * BLOCK, NVEC)


def reference(start, blocks, neighbors, offsets, center, half_width):
    def scaled(vectors):
        return (apply_operator(vectors, blocks, neighbors, offsets) - center[0] * vectors) / half_width[0]

    previous = start
    current = scaled(start)
    for level in range(FILTER - 1):
        following = 2.0 * scaled(current) - previous
        previous, current = current, following
    image = apply_operator(current, blocks, neighbors, offsets)
    gram = jnp.dot(current.T, current, precision=lax.Precision.HIGHEST) / ORBITALS
    projected = jnp.dot(current.T, image, precision=lax.Precision.HIGHEST) / ORBITALS
    return current, gram, projected
```

```python
import functools

import jax
import jax.numpy as jnp
from jax import lax
from jax.experimental import pallas as pl
from jax.experimental.pallas import tpu as pltpu
from jax.sharding import PartitionSpec as P

BLOCK = 128
HALF = 8
ENTRIES = 128
GROUP = 4
PAD = 136
SLOTS = 8
YH, Z, X = 2, 8, 4


def slab_of(y, z, x):
    return (y * Z + z) * X + x


def ring(distance):
    count = YH * Z * X
    return [(i, (i + distance) % count) for i in range(count)]


def slab_pairs(target):
    return [(slab_of(y, z, x), slab_of(*target(y, z, x))) for y in range(YH) for z in range(Z) for x in range(X)]


def device_pairs(target):
    pairs = []
    for s in range(YH * Z * X):
        y, z, x = s // (Z * X), s // X % Z, s % X
        for c in range(4):
            to_x, to_c = target(x, c)
            pairs.append((s * 4 + c, slab_of(y, z, to_x) * 4 + to_c))
    return pairs


def split(value):
    high = value.astype(jnp.bfloat16)
    return high, (value - high.astype(jnp.float32)).astype(jnp.bfloat16)


def sort_kernel(order, *refs):
    out = refs[-1]
    for u in range(GROUP):
        high, low = split(refs[u][0])
        out[u, :, :BLOCK] = high
        out[u, :, BLOCK:] = low


def sorted_blocks(blocks, order):
    spec = lambda u: pl.BlockSpec((1, BLOCK, BLOCK), lambda g, order: (order[g * GROUP + u], 0, 0))
    return pl.pallas_call(
        sort_kernel,
        out_shape=jax.ShapeDtypeStruct((PAD, BLOCK, 2 * BLOCK), jnp.bfloat16),
        grid_spec=pltpu.PrefetchScalarGridSpec(
            num_scalar_prefetch=1,
            grid=(ENTRIES // GROUP,),
            in_specs=[spec(u) for u in range(GROUP)],
            out_specs=pl.BlockSpec((GROUP, BLOCK, 2 * BLOCK), lambda g, order: (g, 0, 0)),
        ),
        cost_estimate=pl.CostEstimate(flops=0, bytes_accessed=16 << 20, transcendentals=0),
        name="sort_blocks",
    )(order, *[blocks] * GROUP)


def accumulate(meta, table, sources, held, chunk, sems, v_sems, acc, first, last, row_base):
    loads = []
    for j, source in enumerate(sources):
        loads.append(pltpu.make_async_copy(source, held.at[pl.ds(j * HALF, HALF)], v_sems.at[j]))
        loads[-1].start()
    groups = lax.div(last - first + (GROUP - 1), GROUP)

    def fetch(k):
        slot = lax.rem(k, SLOTS)
        return pltpu.make_async_copy(table.at[pl.ds(first + k * GROUP, GROUP)], chunk.at[slot], sems.at[slot])

    def prime(k, carry):
        fetch(k).start()
        return carry

    lax.fori_loop(0, jnp.minimum(groups, SLOTS - 1), prime, 0)
    for load in loads:
        load.wait()

    def step(k, carry):
        @pl.when(k + SLOTS - 1 < groups)
        def _():
            fetch(k + SLOTS - 1).start()

        fetch(k).wait()
        slot = lax.rem(k, SLOTS)
        terms, rows = [], []
        for u in range(GROUP):
            e = first + k * GROUP + u
            lhs = chunk[slot, u]
            lhs = jnp.where(e < last, lhs, jnp.zeros_like(lhs))
            high, low = split(held[meta[1, e]])
            term = jnp.dot(lhs, jnp.concatenate([high, high], axis=0), preferred_element_type=jnp.float32)
            term = term + jnp.dot(lhs[:, :BLOCK], low, preferred_element_type=jnp.float32)
            terms.append(term)
            rows.append(meta[0, e] - row_base)
        for u in range(GROUP):
            row = jnp.clip(rows[u], 0, acc.shape[0] - 1)
            acc[row] += terms[u]
        return carry

    lax.fori_loop(0, groups, step, 0)


def near_kernel(meta, table, *refs):
    sources, (acc, held, chunk, sems, v_sems) = refs[:6], refs[6:]
    acc[...] = jnp.zeros_like(acc)
    accumulate(meta, table, sources, held, chunk, sems, v_sems, acc, 0, meta[2, 0], 0)


def scratch(halves):
    return [
        pltpu.VMEM((halves * HALF, BLOCK, BLOCK), jnp.float32),
        pltpu.VMEM((SLOTS, GROUP, BLOCK, 2 * BLOCK), jnp.bfloat16),
        pltpu.SemaphoreType.DMA((SLOTS,)),
        pltpu.SemaphoreType.DMA((halves,)),
    ]


def cost(entries):
    return pl.CostEstimate(flops=entries * 6 * BLOCK**3, bytes_accessed=entries * 4 * BLOCK**2, transcendentals=0)


ANY = pl.BlockSpec(memory_space=pl.ANY)
SMEM = pl.BlockSpec(memory_space=pltpu.SMEM)
VMEM = pl.BlockSpec(memory_space=pltpu.VMEM)


def near_terms(meta, table, sources):
    return pl.pallas_call(
        near_kernel,
        out_shape=jax.ShapeDtypeStruct((2 * HALF, BLOCK, BLOCK), jnp.float32),
        in_specs=[SMEM, ANY] + [ANY] * 6,
        out_specs=VMEM,
        scratch_shapes=scratch(6),
        compiler_params=pltpu.CompilerParams(vmem_limit_bytes=24 << 20),
        cost_estimate=cost(80),
        name="near_terms",
    )(meta, table, *sources)


def far_kernel(half, parts, meta, scale, table, *refs):
    sources, refs = refs[:4], refs[4:]
    near, others, (out, held, chunk, sems, v_sems) = refs[0], refs[1 : 1 + parts], refs[1 + parts :]
    out[...] = near[...]
    first = meta[2, half]
    accumulate(meta, table, sources, held, chunk, sems, v_sems, out, first, meta[2, half + 1], half * HALF)
    if parts:
        value = out[...] * scale[0]
        for j in range(parts):
            value = value + others[j][...] * scale[j + 1]
        out[...] = value


def far_terms(half, meta, scale, table, sources, near, others):
    shape = (HALF, BLOCK, BLOCK)
    return pl.pallas_call(
        functools.partial(far_kernel, half, len(others)),
        out_shape=jax.ShapeDtypeStruct(shape, jnp.float32),
        grid=(1,),
        in_specs=[SMEM, SMEM, ANY] + [ANY] * 4 + [pl.BlockSpec(shape, lambda g: (half, 0, 0))] + [VMEM] * len(others),
        out_specs=VMEM,
        scratch_shapes=scratch(4),
        compiler_params=pltpu.CompilerParams(vmem_limit_bytes=24 << 20),
        cost_estimate=cost(26),
        name="far_terms",
    )(meta, scale, table, *sources, near, *others)


def tables(neighbors, offsets):
    entry = jnp.arange(ENTRIES, dtype=jnp.int32)
    off, nbr = offsets.reshape(ENTRIES), neighbors.reshape(ENTRIES)
    far = jnp.abs(off) == 2
    key = jnp.where(far, ENTRIES, 0) + entry
    rank = jnp.sum((key[None, :] < key[:, None]).astype(jnp.int32), axis=1)
    source = jnp.where(far, jnp.where(off > 0, 2 * HALF, 0), (off + 1) * 2 * HALF) + nbr
    hit = (rank[None, :] == entry[:, None]).astype(jnp.int32)
    order = jnp.sum(hit * entry[None, :], axis=1)
    placed = jnp.sum(hit * source[None, :], axis=1)
    near_count = ENTRIES - jnp.sum(far.astype(jnp.int32))
    middle = near_count + jnp.sum((far & (entry < ENTRIES // 2)).astype(jnp.int32))
    bounds = jnp.stack([near_count, middle, jnp.int32(ENTRIES)])
    widen = lambda v: jnp.pad(v, (0, PAD - v.shape[0]))
    return order, jnp.stack([widen(order // 8), widen(placed), widen(bounds)])


def on_device(start, blocks, neighbors, offsets, center, half_width):
    rows, width = start.shape
    order, meta = tables(neighbors, offsets)
    grid = start.reshape(2 * HALF, BLOCK, width)
    halves = [grid[:HALF], grid[HALF:]]
    slab = lambda value, pairs: lax.ppermute(value, "slab", pairs)

    table = None

    def apply_operator(current, finish):
        nonlocal table
        left = [slab(h, ring(1)) for h in current]
        right = [slab(h, ring(-1)) for h in current]
        far_left = [slab(h, ring(1)) for h in left]
        far_right = [slab(h, ring(-1)) for h in right]
        if table is None:
            table = sorted_blocks(blocks.reshape(ENTRIES, BLOCK, BLOCK), order)
        near = near_terms(meta, table, left + current + right)
        return [finish(h, near, far_left + far_right) for h in range(2)]

    inverse = 1.0 / half_width[0]
    once = jnp.stack([inverse, -center[0] * inverse])
    twice = jnp.stack([2.0 * inverse, -2.0 * center[0] * inverse, jnp.float32(-1.0)])

    previous = halves
    current = apply_operator(halves, lambda h, near, far: far_terms(h, meta, once, table, far, near, [halves[h]]))
    for level in range(2):
        following = apply_operator(
            current, lambda h, near, far: far_terms(h, meta, twice, table, far, near, [current[h], previous[h]])
        )
        previous, current = current, following
    filtered = jnp.concatenate(current, axis=0).reshape(rows, width)

    image = apply_operator(current, lambda h, near, far: far_terms(h, meta, once, table, far, near, []))
    image = jnp.concatenate(image, axis=0).reshape(rows, width)

    across = lax.ppermute(filtered, "col", [(c, c ^ 2) for c in range(4)])
    beside = lax.ppermute(filtered, "col", [(c, c ^ 1) for c in range(4)])
    diagonal = lax.ppermute(across, "col", [(c, c ^ 1) for c in range(4)])
    every = jnp.stack([filtered, beside, across, diagonal])

    col = lax.axis_index("col")
    x = lax.rem(lax.axis_index("slab"), X)
    high = lax.Precision.HIGH
    gram_terms = jnp.einsum("ra,jrb->jab", filtered, every, precision=high)
    image_terms = jnp.einsum("jra,rb->jab", every, image, precision=high)

    gram_own = jnp.take(gram_terms, x, axis=0)
    image_own = None
    for d in range(4):
        sent = jnp.take(image_terms, x ^ d, axis=0)
        got = lax.ppermute(sent, ("slab", "col"), device_pairs(lambda x, c: (x ^ d, c ^ x ^ d)))
        image_own = got if image_own is None else image_own + got
        if d:
            sent = jnp.take(gram_terms, x ^ d, axis=0)
            gram_own = gram_own + slab(sent, slab_pairs(lambda y, z, x: (y, z, x ^ d)))
    own = jnp.stack([gram_own, image_own])
    for moves in (
        [lambda y, z, x, d=d: (y, z ^ d, x) for d in (1, 2, 3)],
        [lambda y, z, x, d=d: (y ^ (d & 1), z ^ ((d >> 1) * 4), x) for d in (1, 2, 3)],
    ):
        arrived = [slab(own, slab_pairs(move)) for move in moves]
        own = own + arrived[0] + (arrived[1] + arrived[2])
    own = own * (1.0 / (rows * YH * Z * X))
    parts = [own] + [slab(own, slab_pairs(lambda y, z, x: (y, z, x ^ d))) for d in (1, 2, 3)]
    stacked = jnp.stack(parts)
    wide = jnp.take(stacked, jnp.arange(4) ^ col ^ x, axis=0)
    gram, projected = (jnp.transpose(wide[:, k], (1, 0, 2)).reshape(BLOCK, 4 * BLOCK) for k in range(2))
    return filtered, gram, projected


def solution(mesh):
    return jax.shard_map(
        on_device,
        mesh=mesh,
        in_specs=(
            P("slab", "col"),
            P("slab", None, None, None),
            P("slab", None),
            P("slab", None),
            P(),
            P(),
        ),
        out_specs=(P("slab", "col"), P("col", None), P("col", None)),
        check_vma=False,
    )
```

```python
import functools

import jax
import jax.numpy as jnp
from jax import lax
from jax.experimental import pallas as pl
from jax.experimental.pallas import tpu as pltpu
from jax.sharding import PartitionSpec as P

BLOCK = 128
BLK = 16
WIDE = 64
ENTRIES = 128
GROUP = 4
SORTED = 16
PAD = ENTRIES + SORTED
SLOTS = 8
YH, Z, X = 2, 8, 4
SLABS = YH * Z * X


def slab_of(y, z, x):
    return (y * Z + z) * X + x


def swaps(first):
    pairs = []
    for s in range(first, SLABS, 2):
        t = (s + 1) % SLABS
        pairs += [(s, t), (t, s)]
    return pairs


def slab_pairs(target):
    return [(slab_of(y, z, x), slab_of(*target(y, z, x))) for y in range(YH) for z in range(Z) for x in range(X)]


def device_pairs(target):
    pairs = []
    for s in range(SLABS):
        y, z, x = s // (Z * X), s // X % Z, s % X
        for c in range(4):
            to_x, to_c = target(x, c)
            pairs.append((s * 4 + c, slab_of(y, z, to_x) * 4 + to_c))
    return pairs


def split(value):
    high = value.astype(jnp.bfloat16)
    return high, (value - high.astype(jnp.float32)).astype(jnp.bfloat16)


def across_lanes(a, b):
    return lax.dot_general(a, b, (((1,), (1,)), ((), ())), preferred_element_type=jnp.float32)


ANY = pl.BlockSpec(memory_space=pl.ANY)
SMEM = pl.BlockSpec(memory_space=pltpu.SMEM)
VMEM = pl.BlockSpec(memory_space=pltpu.VMEM)


def sort_kernel(order, *refs):
    out = refs[-1]
    for u in range(SORTED):
        high, low = split(refs[u][0])
        out[u, :, :BLOCK] = high
        out[u, :, BLOCK:] = low


def sorted_blocks(blocks, order):
    spec = lambda u: pl.BlockSpec((1, BLOCK, BLOCK), lambda g, order: (order[g * SORTED + u], 0, 0))
    return pl.pallas_call(
        sort_kernel,
        out_shape=jax.ShapeDtypeStruct((PAD, BLOCK, 2 * BLOCK), jnp.bfloat16),
        grid_spec=pltpu.PrefetchScalarGridSpec(
            num_scalar_prefetch=1,
            grid=(PAD // SORTED,),
            in_specs=[spec(u) for u in range(SORTED)],
            out_specs=pl.BlockSpec((SORTED, BLOCK, 2 * BLOCK), lambda g, order: (g, 0, 0)),
        ),
        compiler_params=pltpu.CompilerParams(vmem_limit_bytes=16 << 20),
        cost_estimate=pl.CostEstimate(flops=0, bytes_accessed=24 << 20, transcendentals=0),
        name="sort_blocks",
    )(order, *[blocks] * SORTED)


def accumulate(meta, table, sources, held, chunk, sems, v_sems, acc, first, last):
    loads = []
    for j, source in enumerate(sources):
        loads.append(pltpu.make_async_copy(source, held.at[pl.ds(j * BLK, BLK)], v_sems.at[j]))
        loads[-1].start()
    groups = lax.div(last - first + (GROUP - 1), GROUP)

    def fetch(k):
        slot = lax.rem(k, SLOTS)
        return pltpu.make_async_copy(table.at[pl.ds(first + k * GROUP, GROUP)], chunk.at[slot], sems.at[slot])

    def prime(k, carry):
        fetch(k).start()
        return carry

    lax.fori_loop(0, jnp.minimum(groups, SLOTS - 1), prime, 0)
    for load in loads:
        load.wait()

    def step(k, carry):
        @pl.when(k + SLOTS - 1 < groups)
        def _():
            fetch(k + SLOTS - 1).start()

        fetch(k).wait()
        slot = lax.rem(k, SLOTS)
        terms, rows = [], []
        for u in range(GROUP):
            e = first + k * GROUP + u
            value = held[meta[1, e]]
            high, low = split(jnp.where(e < last, value, jnp.zeros_like(value)))
            both = across_lanes(jnp.concatenate([high, low], axis=0), chunk[slot, u, :, :BLOCK])
            terms.append(both[:WIDE] + both[WIDE:] + across_lanes(high, chunk[slot, u, :, BLOCK:]))
            rows.append(meta[0, e])
        for u in range(GROUP):
            acc[rows[u]] += terms[u]
        return carry

    lax.fori_loop(0, groups, step, 0)


HELD = (BLK, WIDE, BLOCK)


def scratch(slabs):
    return [
        pltpu.VMEM((slabs * BLK, WIDE, BLOCK), jnp.float32),
        pltpu.VMEM((SLOTS, GROUP, BLOCK, 2 * BLOCK), jnp.bfloat16),
        pltpu.SemaphoreType.DMA((SLOTS,)),
        pltpu.SemaphoreType.DMA((slabs,)),
    ]


def cost(entries):
    return pl.CostEstimate(flops=entries * 6 * BLOCK**3, bytes_accessed=entries * 4 * BLOCK**2, transcendentals=0)


def near_kernel(meta, table, *refs):
    sources, (acc, held, chunk, sems, v_sems) = refs[:3], refs[3:]
    acc[...] = jnp.zeros_like(acc)
    accumulate(meta, table, sources, held, chunk, sems, v_sems, acc, 0, meta[2, 0])


def near_terms(meta, table, sources):
    return pl.pallas_call(
        near_kernel,
        out_shape=jax.ShapeDtypeStruct(HELD, jnp.float32),
        in_specs=[SMEM, ANY] + [ANY] * 3,
        out_specs=VMEM,
        scratch_shapes=scratch(3),
        compiler_params=pltpu.CompilerParams(vmem_limit_bytes=16 << 20),
        cost_estimate=cost(80),
        name="near_terms",
    )(meta, table, *sources)


def far_kernel(parts, meta, scale, table, *refs):
    sources, near, others, (out, held, chunk, sems, v_sems) = refs[:2], refs[2], refs[3 : 3 + parts], refs[3 + parts :]
    out[...] = near[...]
    accumulate(meta, table, sources, held, chunk, sems, v_sems, out, meta[2, 0], ENTRIES)
    if parts:
        value = out[...] * scale[0]
        for j in range(parts):
            value = value + others[j][...] * scale[j + 1]
        out[...] = value


def far_terms(meta, scale, table, sources, near, others):
    return pl.pallas_call(
        functools.partial(far_kernel, len(others)),
        out_shape=jax.ShapeDtypeStruct(HELD, jnp.float32),
        in_specs=[SMEM, SMEM, ANY] + [ANY] * 2 + [VMEM] * (1 + len(others)),
        out_specs=VMEM,
        scratch_shapes=scratch(2),
        compiler_params=pltpu.CompilerParams(vmem_limit_bytes=16 << 20),
        cost_estimate=cost(52),
        name="far_terms",
    )(meta, scale, table, *sources, near, *others)


def outer_kernel(rows_first, *refs):
    every, right, out, total = refs[:8], refs[8:10], refs[10], refs[11]
    total[...] = jnp.zeros_like(total)

    def step(k, carry):
        def pair(ref):
            return jnp.concatenate([ref[2 * k], ref[2 * k + 1]], axis=-1)

        a = split(jnp.concatenate([pair(ref) for ref in every], axis=0))
        b = split(jnp.concatenate([pair(ref) for ref in right], axis=0))
        if rows_first:
            a, b = b, a
        total[...] += across_lanes(a[0], b[0]) + (across_lanes(a[0], b[1]) + across_lanes(a[1], b[0]))
        return carry

    lax.fori_loop(0, BLK // 2, step, 0)
    for j in range(4):
        part = slice(j * BLOCK, (j + 1) * BLOCK)
        out[j] = total[:, part] if rows_first else total[part, :]


def outer(every, right, rows_first):
    shape = (BLOCK, 4 * BLOCK) if rows_first else (4 * BLOCK, BLOCK)
    return pl.pallas_call(
        functools.partial(outer_kernel, rows_first),
        out_shape=jax.ShapeDtypeStruct((4, BLOCK, BLOCK), jnp.float32),
        in_specs=[VMEM] * 10,
        out_specs=VMEM,
        scratch_shapes=[pltpu.VMEM(shape, jnp.float32)],
        compiler_params=pltpu.CompilerParams(vmem_limit_bytes=24 << 20),
        cost_estimate=pl.CostEstimate(flops=6 * 2048 * 512 * 128, bytes_accessed=6 << 20, transcendentals=0),
        name="outer",
    )(*every, *right)


def tables(neighbors, offsets, odd):
    entry = jnp.arange(ENTRIES, dtype=jnp.int32)
    off, nbr = offsets.reshape(ENTRIES), neighbors.reshape(ENTRIES)
    far = jnp.abs(off) == 2
    key = jnp.where(far, ENTRIES, 0) + entry
    rank = jnp.sum((key[None, :] < key[:, None]).astype(jnp.int32), axis=1)
    by_b = ((off > 0) != odd).astype(jnp.int32)
    source = jnp.where(far, by_b, jnp.where(off == 0, 1, 2 * by_b)) * BLK + nbr
    hit = (rank[None, :] == entry[:, None]).astype(jnp.int32)
    order = jnp.sum(hit * entry[None, :], axis=1)
    placed = jnp.sum(hit * source[None, :], axis=1)
    near_count = ENTRIES - jnp.sum(far.astype(jnp.int32))
    widen = lambda v: jnp.pad(v, (0, PAD - v.shape[0]))
    return widen(order), jnp.stack([widen(order // 8), widen(placed), widen(near_count[None])])


def on_device(start, blocks, neighbors, offsets, center, half_width):
    rows, width = start.shape
    col = lax.axis_index("col")
    x = lax.rem(lax.axis_index("slab"), X)
    order, meta = tables(neighbors, offsets, (x & 1) == 1)
    slab = lambda value, pairs: lax.ppermute(value, "slab", pairs)
    by_a = lambda value: slab(value, swaps(1))
    by_b = lambda value: slab(value, swaps(0))
    table = sorted_blocks(blocks.reshape(ENTRIES, BLOCK, BLOCK), order)

    def apply_operator(current, scale, others):
        result = []
        for h in range(2):
            from_b = by_b(current[h])
            from_a = by_a(current[h])
            far_a = by_a(from_b)
            far_b = by_b(from_a)
            near = near_terms(meta, table, [from_a, current[h], from_b])
            result.append(far_terms(meta, scale, table, [far_a, far_b], near, [o[h] for o in others]))
        return result

    inverse = 1.0 / half_width[0]
    once = jnp.stack([inverse, -center[0] * inverse])
    twice = jnp.stack([2.0 * inverse, -2.0 * center[0] * inverse, jnp.float32(-1.0)])

    grid = jnp.transpose(start.reshape(BLK, BLOCK, width), (0, 2, 1))
    previous = [grid[:, :WIDE], grid[:, WIDE:]]
    current = apply_operator(previous, once, [previous])
    for level in range(2):
        previous, current = current, apply_operator(current, twice, [current, previous])
    image = apply_operator(current, once, [])
    filtered = jnp.transpose(jnp.concatenate(current, axis=1), (0, 2, 1)).reshape(rows, width)

    by_col = lambda value, d: lax.ppermute(value, "col", [(c, c ^ d) for c in range(4)])
    beside = [by_col(h, 1) for h in current]
    across = [by_col(h, 2) for h in current]
    diagonal = [by_col(h, 1) for h in across]
    every = current + beside + across + diagonal

    gram_terms = outer(every, current, True)
    gram_own = jnp.take(gram_terms, x, axis=0)
    for d in (1, 2, 3):
        sent = jnp.take(gram_terms, x ^ d, axis=0)
        gram_own = gram_own + slab(sent, slab_pairs(lambda y, z, x: (y, z, x ^ d)))
    image_terms = outer(every, image, False)
    image_own = None
    for d in range(4):
        sent = jnp.take(image_terms, x ^ d, axis=0)
        got = lax.ppermute(sent, ("slab", "col"), device_pairs(lambda x, c: (x ^ d, c ^ x ^ d)))
        image_own = got if image_own is None else image_own + got
    own = jnp.stack([gram_own, image_own])
    for moves in (
        [lambda y, z, x, d=d: (y, z ^ d, x) for d in (1, 2, 3)],
        [lambda y, z, x, d=d: (y ^ (d & 1), z ^ ((d >> 1) * 4), x) for d in (1, 2, 3)],
    ):
        arrived = [slab(own, slab_pairs(move)) for move in moves]
        own = own + arrived[0] + (arrived[1] + arrived[2])
    own = own * (1.0 / (rows * SLABS))
    parts = [own] + [slab(own, slab_pairs(lambda y, z, x: (y, z, x ^ d))) for d in (1, 2, 3)]
    wide = jnp.take(jnp.stack(parts), jnp.arange(4) ^ col ^ x, axis=0)
    gram, projected = (jnp.transpose(wide[:, k], (1, 0, 2)).reshape(BLOCK, 4 * BLOCK) for k in range(2))
    return filtered, gram, projected


def solution(mesh):
    return jax.shard_map(
        on_device,
        mesh=mesh,
        in_specs=(
            P("slab", "col"),
            P("slab", None, None, None),
            P("slab", None),
            P("slab", None),
            P(),
            P(),
        ),
        out_specs=(P("slab", "col"), P("col", None), P("col", None)),
        check_vma=False,
    )
```

```python
import functools

import jax
import jax.numpy as jnp
from jax import lax
from jax.experimental import pallas as pl
from jax.experimental.pallas import tpu as pltpu
from jax.sharding import PartitionSpec as P

BLOCK = 128
BLK = 16
WIDE = 64
ENTRIES = 128
GROUP = 16
SORTED = 16
PAD = ENTRIES + SORTED
YH, Z, X = 2, 8, 4
SLABS = YH * Z * X


def slab_of(y, z, x):
    return (y * Z + z) * X + x


def swaps(first):
    pairs = []
    for s in range(first, SLABS, 2):
        t = (s + 1) % SLABS
        pairs += [(s, t), (t, s)]
    return pairs


def slab_pairs(target):
    return [(slab_of(y, z, x), slab_of(*target(y, z, x))) for y in range(YH) for z in range(Z) for x in range(X)]


def device_pairs(target):
    pairs = []
    for s in range(SLABS):
        y, z, x = s // (Z * X), s // X % Z, s % X
        for c in range(4):
            to_x, to_c = target(x, c)
            pairs.append((s * 4 + c, slab_of(y, z, to_x) * 4 + to_c))
    return pairs


def split(value):
    high = value.astype(jnp.bfloat16)
    return high, (value - high.astype(jnp.float32)).astype(jnp.bfloat16)


def across_lanes(a, b):
    return lax.dot_general(a, b, (((1,), (1,)), ((), ())), preferred_element_type=jnp.float32)


ANY = pl.BlockSpec(memory_space=pl.ANY)
SMEM = pl.BlockSpec(memory_space=pltpu.SMEM)
VMEM = pl.BlockSpec(memory_space=pltpu.VMEM)


def sort_kernel(order, *refs):
    out = refs[-1]
    for u in range(SORTED):
        high, low = split(refs[u][0])
        out[u, :, :BLOCK] = high
        out[u, :, BLOCK:] = low


def sorted_blocks(blocks, order):
    spec = lambda u: pl.BlockSpec((1, BLOCK, BLOCK), lambda g, order: (order[g * SORTED + u], 0, 0))
    return pl.pallas_call(
        sort_kernel,
        out_shape=jax.ShapeDtypeStruct((PAD, BLOCK, 2 * BLOCK), jnp.bfloat16),
        grid_spec=pltpu.PrefetchScalarGridSpec(
            num_scalar_prefetch=1,
            grid=(PAD // SORTED,),
            in_specs=[spec(u) for u in range(SORTED)],
            out_specs=pl.BlockSpec((SORTED, BLOCK, 2 * BLOCK), lambda g, order: (g, 0, 0)),
        ),
        compiler_params=pltpu.CompilerParams(vmem_limit_bytes=16 << 20),
        cost_estimate=pl.CostEstimate(flops=0, bytes_accessed=24 << 20, transcendentals=0),
        name="sort_blocks",
    )(order, *[blocks] * SORTED)


def accumulate(meta, table, sources, held, sems, acc, first, last):
    loads = []
    for j, source in enumerate(sources):
        loads.append(pltpu.make_async_copy(source, held.at[pl.ds(j * BLK, BLK)], sems.at[j]))
        loads[-1].start()
    for load in loads:
        load.wait()

    def step(k, carry):
        terms, rows = [], []
        for u in range(GROUP):
            e = first + k * GROUP + u
            value = held[meta[1, e]]
            high, low = split(jnp.where(e < last, value, jnp.zeros_like(value)))
            lhs = jnp.concatenate(
                [jnp.concatenate([high, high], axis=1), jnp.concatenate([low, jnp.zeros_like(low)], axis=1)], axis=0
            )
            both = across_lanes(lhs, table[e])
            terms.append(both[:WIDE] + both[WIDE:])
            rows.append(meta[0, e])
        for u in range(GROUP):
            acc[rows[u]] += terms[u]
        return carry

    lax.fori_loop(0, lax.div(last - first + (GROUP - 1), GROUP), step, 0)


HELD = (BLK, WIDE, BLOCK)


def scratch(slabs):
    return [
        pltpu.VMEM((slabs * BLK, WIDE, BLOCK), jnp.float32),
        pltpu.SemaphoreType.DMA((slabs,)),
    ]


def cost(entries):
    return pl.CostEstimate(flops=entries * 6 * BLOCK**3, bytes_accessed=entries * 4 * BLOCK**2, transcendentals=0)


def near_kernel(meta, table, *refs):
    sources, (acc, held, sems) = refs[:3], refs[3:]
    acc[...] = jnp.zeros_like(acc)
    accumulate(meta, table, sources, held, sems, acc, 0, meta[2, 0])


def near_terms(meta, table, sources):
    return pl.pallas_call(
        near_kernel,
        out_shape=jax.ShapeDtypeStruct(HELD, jnp.float32),
        in_specs=[SMEM, VMEM] + [ANY] * 3,
        out_specs=VMEM,
        scratch_shapes=scratch(3),
        compiler_params=pltpu.CompilerParams(vmem_limit_bytes=24 << 20),
        cost_estimate=cost(80),
        name="near_terms",
    )(meta, table, *sources)


def far_kernel(parts, meta, scale, table, *refs):
    sources, near, others, (out, held, sems) = refs[:2], refs[2], refs[3 : 3 + parts], refs[3 + parts :]
    out[...] = near[...]
    accumulate(meta, table, sources, held, sems, out, meta[2, 0], ENTRIES)
    if parts:
        value = out[...] * scale[0]
        for j in range(parts):
            value = value + others[j][...] * scale[j + 1]
        out[...] = value


def far_terms(meta, scale, table, sources, near, others):
    return pl.pallas_call(
        functools.partial(far_kernel, len(others)),
        out_shape=jax.ShapeDtypeStruct(HELD, jnp.float32),
        in_specs=[SMEM, SMEM, VMEM] + [ANY] * 2 + [VMEM] * (1 + len(others)),
        out_specs=VMEM,
        scratch_shapes=scratch(2),
        compiler_params=pltpu.CompilerParams(vmem_limit_bytes=24 << 20),
        cost_estimate=cost(52),
        name="far_terms",
    )(meta, scale, table, *sources, near, *others)


def outer_kernel(rows_first, *refs):
    every, right, out, total = refs[:8], refs[8:10], refs[10], refs[11]
    total[...] = jnp.zeros_like(total)

    def step(k, carry):
        def pair(ref):
            return jnp.concatenate([ref[2 * k], ref[2 * k + 1]], axis=-1)

        a = split(jnp.concatenate([pair(ref) for ref in every], axis=0))
        b = split(jnp.concatenate([pair(ref) for ref in right], axis=0))
        if rows_first:
            a, b = b, a
        total[...] += across_lanes(a[0], b[0]) + (across_lanes(a[0], b[1]) + across_lanes(a[1], b[0]))
        return carry

    lax.fori_loop(0, BLK // 2, step, 0)
    for j in range(4):
        part = slice(j * BLOCK, (j + 1) * BLOCK)
        out[j] = total[:, part] if rows_first else total[part, :]


def outer(every, right, rows_first):
    shape = (BLOCK, 4 * BLOCK) if rows_first else (4 * BLOCK, BLOCK)
    return pl.pallas_call(
        functools.partial(outer_kernel, rows_first),
        out_shape=jax.ShapeDtypeStruct((4, BLOCK, BLOCK), jnp.float32),
        in_specs=[VMEM] * 10,
        out_specs=VMEM,
        scratch_shapes=[pltpu.VMEM(shape, jnp.float32)],
        compiler_params=pltpu.CompilerParams(vmem_limit_bytes=24 << 20),
        cost_estimate=pl.CostEstimate(flops=6 * 2048 * 512 * 128, bytes_accessed=6 << 20, transcendentals=0),
        name="outer",
    )(*every, *right)


def tables(neighbors, offsets, odd):
    entry = jnp.arange(ENTRIES, dtype=jnp.int32)
    off, nbr = offsets.reshape(ENTRIES), neighbors.reshape(ENTRIES)
    far = jnp.abs(off) == 2
    key = jnp.where(far, ENTRIES, 0) + entry
    rank = jnp.sum((key[None, :] < key[:, None]).astype(jnp.int32), axis=1)
    by_b = ((off > 0) != odd).astype(jnp.int32)
    source = jnp.where(far, by_b, jnp.where(off == 0, 1, 2 * by_b)) * BLK + nbr
    hit = (rank[None, :] == entry[:, None]).astype(jnp.int32)
    order = jnp.sum(hit * entry[None, :], axis=1)
    placed = jnp.sum(hit * source[None, :], axis=1)
    near_count = ENTRIES - jnp.sum(far.astype(jnp.int32))
    widen = lambda v: jnp.pad(v, (0, PAD - v.shape[0]))
    return widen(order), jnp.stack([widen(order // 8), widen(placed), widen(near_count[None])])


def on_device(start, blocks, neighbors, offsets, center, half_width):
    rows, width = start.shape
    col = lax.axis_index("col")
    x = lax.rem(lax.axis_index("slab"), X)
    order, meta = tables(neighbors, offsets, (x & 1) == 1)
    slab = lambda value, pairs: lax.ppermute(value, "slab", pairs)
    by_a = lambda value: slab(value, swaps(1))
    by_b = lambda value: slab(value, swaps(0))
    table = sorted_blocks(blocks.reshape(ENTRIES, BLOCK, BLOCK), order)

    def near_and_far(value):
        from_b = by_b(value)
        from_a = by_a(value)
        far = [by_a(from_b), by_b(from_a)]
        return near_terms(meta, table, [from_a, value, from_b]), far

    def apply_operator(current, scale, others):
        result = []
        for h in range(2):
            near, far = near_and_far(current[h])
            result.append(far_terms(meta, scale, table, far, near, [o[h] for o in others]))
        return result

    inverse = 1.0 / half_width[0]
    once = jnp.stack([inverse, -center[0] * inverse])
    twice = jnp.stack([2.0 * inverse, -2.0 * center[0] * inverse, jnp.float32(-1.0)])

    grid = jnp.transpose(start.reshape(BLK, BLOCK, width), (0, 2, 1))
    previous = [grid[:, :WIDE], grid[:, WIDE:]]
    current = apply_operator(previous, once, [previous])
    for level in range(2):
        previous, current = current, apply_operator(current, twice, [current, previous])
    parts = [near_and_far(h) for h in current]
    near = [part[0] for part in parts]
    filtered = jnp.transpose(jnp.concatenate(current, axis=1), (0, 2, 1)).reshape(rows, width)

    by_col = lambda value, d: lax.ppermute(value, "col", [(c, c ^ d) for c in range(4)])
    beside = [by_col(h, 1) for h in current]
    across = [by_col(h, 2) for h in current]
    across, near = lax.optimization_barrier((across, near))
    diagonal = [by_col(h, 1) for h in across]
    every = current + beside + across + diagonal

    gram_terms = outer(every, current, True)
    gram_own = jnp.take(gram_terms, x, axis=0)
    for d in (1, 2, 3):
        sent = jnp.take(gram_terms, x ^ d, axis=0)
        gram_own = gram_own + slab(sent, slab_pairs(lambda y, z, x: (y, z, x ^ d)))
    image = [far_terms(meta, once, table, part[1], near[h], []) for h, part in enumerate(parts)]
    image_terms = outer(every, image, False)
    image_own = None
    for d in range(4):
        sent = jnp.take(image_terms, x ^ d, axis=0)
        got = lax.ppermute(sent, ("slab", "col"), device_pairs(lambda x, c: (x ^ d, c ^ x ^ d)))
        image_own = got if image_own is None else image_own + got
    q = lax.rem(lax.div(lax.axis_index("slab"), X), 4)
    beside_z = [slab_pairs(lambda y, z, x, d=d: (y, z ^ d, x)) for d in (1, 2, 3)]
    apart = [slab_pairs(lambda y, z, x, d=d: (y ^ (d & 1), z ^ ((d >> 1) * 4), x)) for d in (1, 2, 3)]
    whole = jnp.stack([gram_own, image_own]).reshape(2, 4, BLOCK // 4, BLOCK)
    own = jnp.take(whole, q, axis=1)
    arrived = [slab(jnp.take(whole, q ^ d, axis=1), pairs) for d, pairs in zip((1, 2, 3), beside_z)]
    own = own + arrived[0] + (arrived[1] + arrived[2])
    arrived = [slab(own, pairs) for pairs in apart]
    own = own + arrived[0] + (arrived[1] + arrived[2])
    own = own * (1.0 / (rows * SLABS))
    quarters = jnp.stack([own] + [slab(own, pairs) for pairs in beside_z], axis=1)
    own = jnp.take(quarters, jnp.arange(4) ^ q, axis=1).reshape(2, BLOCK, BLOCK)
    parts = [own] + [slab(own, slab_pairs(lambda y, z, x: (y, z, x ^ d))) for d in (1, 2, 3)]
    wide = jnp.take(jnp.stack(parts), jnp.arange(4) ^ col ^ x, axis=0)
    gram, projected = (jnp.transpose(wide[:, k], (1, 0, 2)).reshape(BLOCK, 4 * BLOCK) for k in range(2))
    return filtered, gram, projected


def solution(mesh):
    return jax.shard_map(
        on_device,
        mesh=mesh,
        in_specs=(
            P("slab", "col"),
            P("slab", None, None, None),
            P("slab", None),
            P("slab", None),
            P(),
            P(),
        ),
        out_specs=(P("slab", "col"), P("col", None), P("col", None)),
        check_vma=False,
    )
```

```python
import functools

import jax
import jax.numpy as jnp
from jax import lax
from jax.experimental import pallas as pl
from jax.experimental.pallas import tpu as pltpu
from jax.sharding import PartitionSpec as P

BLOCK = 128
BLK = 16
WIDE = 64
ENTRIES = 128
GROUP = 16
SORTED = 16
PAD = ENTRIES + SORTED
YH, Z, X = 2, 8, 4
SLABS = YH * Z * X


def slab_of(y, z, x):
    return (y * Z + z) * X + x


def swaps(first):
    pairs = []
    for s in range(first, SLABS, 2):
        t = (s + 1) % SLABS
        pairs += [(s, t), (t, s)]
    return pairs


def slab_pairs(target):
    return [(slab_of(y, z, x), slab_of(*target(y, z, x))) for y in range(YH) for z in range(Z) for x in range(X)]


def device_pairs(target):
    pairs = []
    for s in range(SLABS):
        y, z, x = s // (Z * X), s // X % Z, s % X
        for c in range(4):
            to_x, to_c = target(x, c)
            pairs.append((s * 4 + c, slab_of(y, z, to_x) * 4 + to_c))
    return pairs


def split(value):
    high = value.astype(jnp.bfloat16)
    return high, (value - high.astype(jnp.float32)).astype(jnp.bfloat16)


def across_lanes(a, b):
    return lax.dot_general(a, b, (((1,), (1,)), ((), ())), preferred_element_type=jnp.float32)


ANY = pl.BlockSpec(memory_space=pl.ANY)
SMEM = pl.BlockSpec(memory_space=pltpu.SMEM)
VMEM = pl.BlockSpec(memory_space=pltpu.VMEM)


def sort_kernel(order, *refs):
    out = refs[-1]
    for u in range(SORTED):
        high, low = split(refs[u][0])
        out[u, :, :BLOCK] = high
        out[u, :, BLOCK:] = low


def sorted_blocks(blocks, order):
    spec = lambda u: pl.BlockSpec((1, BLOCK, BLOCK), lambda g, order: (order[g * SORTED + u], 0, 0))
    return pl.pallas_call(
        sort_kernel,
        out_shape=jax.ShapeDtypeStruct((PAD, BLOCK, 2 * BLOCK), jnp.bfloat16),
        grid_spec=pltpu.PrefetchScalarGridSpec(
            num_scalar_prefetch=1,
            grid=(PAD // SORTED,),
            in_specs=[spec(u) for u in range(SORTED)],
            out_specs=pl.BlockSpec((SORTED, BLOCK, 2 * BLOCK), lambda g, order: (g, 0, 0)),
        ),
        compiler_params=pltpu.CompilerParams(vmem_limit_bytes=16 << 20),
        cost_estimate=pl.CostEstimate(flops=0, bytes_accessed=24 << 20, transcendentals=0),
        name="sort_blocks",
    )(order, *[blocks] * SORTED)


def accumulate(meta, table, sources, held, sems, acc, first, last):
    loads = []
    for j, source in enumerate(sources):
        loads.append(pltpu.make_async_copy(source, held.at[pl.ds(j * BLK, BLK)], sems.at[j]))
        loads[-1].start()
    for load in loads:
        load.wait()

    def step(k, carry):
        terms, rows = [], []
        for u in range(GROUP):
            e = first + k * GROUP + u
            value = held[meta[1, e]]
            high, low = split(jnp.where(e < last, value, jnp.zeros_like(value)))
            lhs = jnp.concatenate(
                [jnp.concatenate([high, high], axis=1), jnp.concatenate([low, jnp.zeros_like(low)], axis=1)], axis=0
            )
            both = across_lanes(lhs, table[e])
            terms.append(both[:WIDE] + both[WIDE:])
            rows.append(meta[0, e])
        for u in range(GROUP):
            acc[rows[u]] += terms[u]
        return carry

    lax.fori_loop(0, lax.div(last - first + (GROUP - 1), GROUP), step, 0)


HELD = (BLK, WIDE, BLOCK)


def scratch(slabs):
    return [
        pltpu.VMEM((slabs * BLK, WIDE, BLOCK), jnp.float32),
        pltpu.SemaphoreType.DMA((slabs,)),
    ]


def cost(entries):
    return pl.CostEstimate(flops=entries * 6 * BLOCK**3, bytes_accessed=entries * 4 * BLOCK**2, transcendentals=0)


def near_kernel(meta, table, *refs):
    sources, (acc, held, sems) = refs[:3], refs[3:]
    acc[...] = jnp.zeros_like(acc)
    accumulate(meta, table, sources, held, sems, acc, 0, meta[2, 0])


def near_terms(meta, table, sources):
    return pl.pallas_call(
        near_kernel,
        out_shape=jax.ShapeDtypeStruct(HELD, jnp.float32),
        in_specs=[SMEM, VMEM] + [ANY] * 3,
        out_specs=VMEM,
        scratch_shapes=scratch(3),
        compiler_params=pltpu.CompilerParams(vmem_limit_bytes=16 << 20),
        cost_estimate=cost(80),
        name="near_terms",
    )(meta, table, *sources)


def far_kernel(parts, meta, scale, table, *refs):
    sources, near, others, (out, held, sems) = refs[:2], refs[2], refs[3 : 3 + parts], refs[3 + parts :]
    out[...] = near[...]
    accumulate(meta, table, sources, held, sems, out, meta[2, 0], ENTRIES)
    if parts:
        value = out[...] * scale[0]
        for j in range(parts):
            value = value + others[j][...] * scale[j + 1]
        out[...] = value


def far_terms(meta, scale, table, sources, near, others):
    return pl.pallas_call(
        functools.partial(far_kernel, len(others)),
        out_shape=jax.ShapeDtypeStruct(HELD, jnp.float32),
        in_specs=[SMEM, SMEM, VMEM] + [ANY] * 2 + [VMEM] * (1 + len(others)),
        out_specs=VMEM,
        scratch_shapes=scratch(2),
        compiler_params=pltpu.CompilerParams(vmem_limit_bytes=16 << 20),
        cost_estimate=cost(52),
        name="far_terms",
    )(meta, scale, table, *sources, near, *others)


def outer_kernel(*refs):
    every = [ref.at[h] for ref in refs[:4] for h in range(2)]
    right, out, total = every[:2] + list(refs[4:6]), refs[6], refs[7]
    total[...] = jnp.zeros_like(total)

    def step(k, carry):
        def some(ref):
            return jnp.concatenate([ref[4 * k + i] for i in range(4)], axis=-1)

        a = split(jnp.concatenate([some(ref) for ref in every], axis=0))
        b = split(jnp.concatenate([some(ref) for ref in right], axis=0))
        total[...] += across_lanes(a[0], b[0]) + (across_lanes(a[0], b[1]) + across_lanes(a[1], b[0]))
        return carry

    lax.fori_loop(0, BLK // 4, step, 0)
    for j in range(4):
        for k in range(2):
            out[j, k] = total[j * BLOCK : (j + 1) * BLOCK, k * BLOCK : (k + 1) * BLOCK]


def outer(every, image):
    return pl.pallas_call(
        outer_kernel,
        out_shape=jax.ShapeDtypeStruct((4, 2, BLOCK, BLOCK), jnp.float32),
        in_specs=[VMEM] * 6,
        out_specs=VMEM,
        scratch_shapes=[pltpu.VMEM((4 * BLOCK, 2 * BLOCK), jnp.float32)],
        compiler_params=pltpu.CompilerParams(vmem_limit_bytes=16 << 20),
        cost_estimate=pl.CostEstimate(flops=6 * 2048 * 512 * 256, bytes_accessed=6 << 20, transcendentals=0),
        name="outer",
    )(*every, *image)


def place_kernel(place, *refs):
    for d in range(4):
        columns = pl.ds(pl.multiple_of(place[d] * BLOCK, BLOCK), BLOCK)
        for k in range(2):
            refs[4 + k][:, columns] = refs[d][k]


def placed_columns(place, parts):
    return pl.pallas_call(
        place_kernel,
        out_shape=[jax.ShapeDtypeStruct((BLOCK, 4 * BLOCK), jnp.float32)] * 2,
        in_specs=[SMEM] + [VMEM] * 4,
        out_specs=[VMEM] * 2,
        compiler_params=pltpu.CompilerParams(vmem_limit_bytes=4 << 20),
        name="place",
    )(place, *parts)


def tables(neighbors, offsets, odd):
    entry = jnp.arange(ENTRIES, dtype=jnp.int32)
    off, nbr = offsets.reshape(ENTRIES), neighbors.reshape(ENTRIES)
    far = jnp.abs(off) == 2
    key = jnp.where(far, ENTRIES, 0) + entry
    rank = jnp.sum((key[None, :] < key[:, None]).astype(jnp.int32), axis=1)
    by_b = ((off > 0) != odd).astype(jnp.int32)
    source = jnp.where(far, by_b, jnp.where(off == 0, 1, 2 * by_b)) * BLK + nbr
    hit = (rank[None, :] == entry[:, None]).astype(jnp.int32)
    order = jnp.sum(hit * entry[None, :], axis=1)
    placed = jnp.sum(hit * source[None, :], axis=1)
    near_count = ENTRIES - jnp.sum(far.astype(jnp.int32))
    widen = lambda v: jnp.pad(v, (0, PAD - v.shape[0]))
    return widen(order), jnp.stack([widen(order // 8), widen(placed), widen(near_count[None])])


def on_device(start, blocks, neighbors, offsets, center, half_width):
    rows, width = start.shape
    col = lax.axis_index("col")
    x = lax.rem(lax.axis_index("slab"), X)
    order, meta = tables(neighbors, offsets, (x & 1) == 1)
    slab = lambda value, pairs: lax.ppermute(value, "slab", pairs)
    by_a = lambda value: slab(value, swaps(1))
    by_b = lambda value: slab(value, swaps(0))
    table = sorted_blocks(blocks.reshape(ENTRIES, BLOCK, BLOCK), order)

    def near_and_far(value):
        from_b = by_b(value)
        from_a = by_a(value)
        far = [by_a(from_b), by_b(from_a)]
        return near_terms(meta, table, [from_a, value, from_b]), far, [from_a, from_b]

    def apply_operator(current, scale, others):
        result = []
        for h in range(2):
            near, far, _ = near_and_far(current[h])
            result.append(far_terms(meta, scale, table, far, near, [o[h] for o in others]))
        return result

    inverse = 1.0 / half_width[0]
    once = jnp.stack([inverse, -center[0] * inverse])
    twice = jnp.stack([2.0 * inverse, -2.0 * center[0] * inverse, jnp.float32(-1.0)])

    grid = jnp.transpose(start.reshape(BLK, BLOCK, width), (0, 2, 1))
    previous = [grid[:, :WIDE], grid[:, WIDE:]]
    current = apply_operator(previous, once, [previous])
    for level in range(2):
        previous, current = current, apply_operator(current, twice, [current, previous])
    parts = [near_and_far(h) for h in current]
    filtered = jnp.transpose(jnp.concatenate(current, axis=1), (0, 2, 1)).reshape(rows, width)

    by_col = lambda value, d: lax.ppermute(value, "col", [(c, c ^ d) for c in range(4)])
    beside = [by_col(h, 1) for h in current]
    both, _ = lax.optimization_barrier((jnp.stack(current), [part[2] for part in parts]))
    across = by_col(both, 2)
    across, far, near = lax.optimization_barrier((across, [part[1] for part in parts], [part[0] for part in parts]))
    every = [both, by_col(both, 1), across, by_col(across, 1)]
    image = [far_terms(meta, once, table, far[h], near[h], []) for h in range(2)]

    terms = outer(every, image)
    own = None
    for d in range(4):
        sent = jnp.take(terms, x ^ d, axis=0)
        got = lax.ppermute(sent, ("slab", "col"), device_pairs(lambda x, c: (x ^ d, c ^ x ^ d)))
        own = got if own is None else own + got
    q = lax.rem(lax.div(lax.axis_index("slab"), X), 4)
    beside_z = [slab_pairs(lambda y, z, x, d=d: (y, z ^ d, x)) for d in (1, 2, 3)]
    whole = own.reshape(2, 4, BLOCK // 4, BLOCK)
    own = jnp.take(whole, q, axis=1)
    arrived = [slab(jnp.take(whole, q ^ d, axis=1), pairs) for d, pairs in zip((1, 2, 3), beside_z)]
    own = own + arrived[0] + (arrived[1] + arrived[2])
    own = own + slab(own, slab_pairs(lambda y, z, x: (y, z ^ 4, x)))
    own = own + slab(own, slab_pairs(lambda y, z, x: (y ^ 1, z, x)))
    own = own * (1.0 / (rows * SLABS))
    quarters = jnp.stack([own] + [slab(own, pairs) for pairs in beside_z], axis=1)
    own = jnp.take(quarters, jnp.arange(4) ^ q, axis=1).reshape(2, BLOCK, BLOCK)
    parts = [own] + [slab(own, slab_pairs(lambda y, z, x: (y, z, x ^ d))) for d in (1, 2, 3)]
    gram, projected = placed_columns(col ^ x ^ jnp.arange(4), parts)
    return filtered, gram, projected


def solution(mesh):
    return jax.shard_map(
        on_device,
        mesh=mesh,
        in_specs=(
            P("slab", "col"),
            P("slab", None, None, None),
            P("slab", None),
            P("slab", None),
            P(),
            P(),
        ),
        out_specs=(P("slab", "col"), P("col", None), P("col", None)),
        check_vma=False,
    )
```

```python
import functools

import jax
import jax.numpy as jnp
from jax import lax
from jax.experimental import pallas as pl
from jax.experimental.pallas import tpu as pltpu
from jax.sharding import PartitionSpec as P

BLOCK = 128
BLK = 16
WIDE = 64
ENTRIES = 128
GROUP = 16
SORTED = 16
PAD = ENTRIES + SORTED
YH, Z, X = 2, 8, 4
SLABS = YH * Z * X


def slab_of(y, z, x):
    return (y * Z + z) * X + x


def swaps(first):
    pairs = []
    for s in range(first, SLABS, 2):
        t = (s + 1) % SLABS
        pairs += [(s, t), (t, s)]
    return pairs


def slab_pairs(target):
    return [(slab_of(y, z, x), slab_of(*target(y, z, x))) for y in range(YH) for z in range(Z) for x in range(X)]


def device_pairs(target):
    pairs = []
    for s in range(SLABS):
        y, z, x = s // (Z * X), s // X % Z, s % X
        for c in range(4):
            to_x, to_c = target(x, c)
            pairs.append((s * 4 + c, slab_of(y, z, to_x) * 4 + to_c))
    return pairs


def split(value):
    high = value.astype(jnp.bfloat16)
    return high, (value - high.astype(jnp.float32)).astype(jnp.bfloat16)


def across_lanes(a, b):
    return lax.dot_general(a, b, (((1,), (1,)), ((), ())), preferred_element_type=jnp.float32)


ANY = pl.BlockSpec(memory_space=pl.ANY)
SMEM = pl.BlockSpec(memory_space=pltpu.SMEM)
VMEM = pl.BlockSpec(memory_space=pltpu.VMEM)


def sort_kernel(order, *refs):
    out = refs[-1]
    for u in range(SORTED):
        high, low = split(refs[u][0])
        out[u, :, :BLOCK] = high
        out[u, :, BLOCK:] = low


def sorted_blocks(blocks, order):
    spec = lambda u: pl.BlockSpec((1, BLOCK, BLOCK), lambda g, order: (order[g * SORTED + u], 0, 0))
    return pl.pallas_call(
        sort_kernel,
        out_shape=jax.ShapeDtypeStruct((PAD, BLOCK, 2 * BLOCK), jnp.bfloat16),
        grid_spec=pltpu.PrefetchScalarGridSpec(
            num_scalar_prefetch=1,
            grid=(PAD // SORTED,),
            in_specs=[spec(u) for u in range(SORTED)],
            out_specs=pl.BlockSpec((SORTED, BLOCK, 2 * BLOCK), lambda g, order: (g, 0, 0)),
        ),
        compiler_params=pltpu.CompilerParams(vmem_limit_bytes=16 << 20),
        cost_estimate=pl.CostEstimate(flops=0, bytes_accessed=24 << 20, transcendentals=0),
        name="sort_blocks",
    )(order, *[blocks] * SORTED)


def accumulate(meta, table, sources, held, sems, acc, first, last):
    loads = []
    for j, source in enumerate(sources):
        loads.append(pltpu.make_async_copy(source, held.at[pl.ds(j * BLK, BLK)], sems.at[j]))
        loads[-1].start()
    for load in loads:
        load.wait()

    def step(k, carry):
        terms, rows = [], []
        for u in range(GROUP):
            e = first + k * GROUP + u
            value = held[meta[1, e]]
            high, low = split(jnp.where(e < last, value, jnp.zeros_like(value)))
            lhs = jnp.concatenate(
                [jnp.concatenate([high, high], axis=1), jnp.concatenate([low, jnp.zeros_like(low)], axis=1)], axis=0
            )
            both = across_lanes(lhs, table[e])
            terms.append(both[:WIDE] + both[WIDE:])
            rows.append(meta[0, e])
        for u in range(GROUP):
            acc[rows[u]] += terms[u]
        return carry

    lax.fori_loop(0, lax.div(last - first + (GROUP - 1), GROUP), step, 0)


HELD = (BLK, WIDE, BLOCK)


def scratch(slabs):
    return [
        pltpu.VMEM((slabs * BLK, WIDE, BLOCK), jnp.float32),
        pltpu.SemaphoreType.DMA((slabs,)),
    ]


def cost(entries):
    return pl.CostEstimate(flops=entries * 6 * BLOCK**3, bytes_accessed=entries * 4 * BLOCK**2, transcendentals=0)


def near_kernel(meta, table, *refs):
    sources, (acc, held, sems) = refs[:3], refs[3:]
    acc[...] = jnp.zeros_like(acc)
    accumulate(meta, table, sources, held, sems, acc, 0, meta[2, 0])


def near_terms(meta, table, sources):
    return pl.pallas_call(
        near_kernel,
        out_shape=jax.ShapeDtypeStruct(HELD, jnp.float32),
        in_specs=[SMEM, VMEM] + [ANY] * 3,
        out_specs=VMEM,
        scratch_shapes=scratch(3),
        compiler_params=pltpu.CompilerParams(vmem_limit_bytes=16 << 20),
        cost_estimate=cost(80),
        name="near_terms",
    )(meta, table, *sources)


def far_kernel(parts, meta, scale, table, *refs):
    sources, near, others, (out, held, sems) = refs[:2], refs[2], refs[3 : 3 + parts], refs[3 + parts :]
    out[...] = near[...]
    accumulate(meta, table, sources, held, sems, out, meta[2, 0], ENTRIES)
    if parts:
        value = out[...] * scale[0]
        for j in range(parts):
            value = value + others[j][...] * scale[j + 1]
        out[...] = value


def far_terms(meta, scale, table, sources, near, others):
    return pl.pallas_call(
        functools.partial(far_kernel, len(others)),
        out_shape=jax.ShapeDtypeStruct(HELD, jnp.float32),
        in_specs=[SMEM, SMEM, VMEM] + [ANY] * 2 + [VMEM] * (1 + len(others)),
        out_specs=VMEM,
        scratch_shapes=scratch(2),
        compiler_params=pltpu.CompilerParams(vmem_limit_bytes=16 << 20),
        cost_estimate=cost(52),
        name="far_terms",
    )(meta, scale, table, *sources, near, *others)


def outer_kernel(meta, *refs):
    every = [ref.at[h] for ref in refs[:4] for h in range(2)]
    right, outs, total = every[:2] + list(refs[4:6]), refs[6:10], refs[10]
    total[...] = jnp.zeros_like(total)

    def step(k, carry):
        def some(ref):
            return jnp.concatenate([ref[4 * k + i] for i in range(4)], axis=-1)

        a = split(jnp.concatenate([some(ref) for ref in every], axis=0))
        b = split(jnp.concatenate([some(ref) for ref in right], axis=0))
        total[...] += across_lanes(a[0], b[0]) + (across_lanes(a[0], b[1]) + across_lanes(a[1], b[0]))
        return carry

    lax.fori_loop(0, BLK // 4, step, 0)
    for d in range(4):
        part = pl.ds(pl.multiple_of((meta[2, 1] ^ d) * BLOCK, BLOCK), BLOCK)
        for k in range(2):
            outs[d][k] = total[part, k * BLOCK : (k + 1) * BLOCK]


def outer(meta, every, image):
    return pl.pallas_call(
        outer_kernel,
        out_shape=[jax.ShapeDtypeStruct((2, BLOCK, BLOCK), jnp.float32)] * 4,
        in_specs=[SMEM] + [VMEM] * 6,
        out_specs=[VMEM] * 4,
        scratch_shapes=[pltpu.VMEM((4 * BLOCK, 2 * BLOCK), jnp.float32)],
        compiler_params=pltpu.CompilerParams(vmem_limit_bytes=12 << 20),
        cost_estimate=pl.CostEstimate(flops=6 * 2048 * 512 * 256, bytes_accessed=6 << 20, transcendentals=0),
        name="outer",
    )(meta, *every, *image)


PART = BLOCK // 4


def small(kernel, outs, meta, parts, name):
    return pl.pallas_call(
        kernel,
        out_shape=[jax.ShapeDtypeStruct(shape, jnp.float32) for shape in outs],
        in_specs=[SMEM] + [VMEM] * len(parts),
        out_specs=[VMEM] * len(outs),
        compiler_params=pltpu.CompilerParams(vmem_limit_bytes=4 << 20),
        name=name,
    )(meta, *parts)


def quarter(meta, d):
    return pl.ds(pl.multiple_of((meta[2, 2] ^ d) * PART, PART), PART)


def scatter_kernel(meta, *refs):
    for d in range(4):
        part = quarter(meta, d)
        for k in range(2):
            refs[4 + d][k] = (refs[0][k, part] + refs[1][k, part]) + (refs[2][k, part] + refs[3][k, part])


def gather_kernel(meta, *refs):
    for d in range(4):
        for k in range(2):
            refs[4][k, quarter(meta, d)] = refs[d][k]


def place_kernel(meta, *refs):
    for d in range(4):
        columns = pl.ds(pl.multiple_of((meta[2, 3] ^ d) * BLOCK, BLOCK), BLOCK)
        for k in range(2):
            refs[4 + k][:, columns] = refs[d][k]


def tables(neighbors, offsets, x, q, col):
    entry = jnp.arange(ENTRIES, dtype=jnp.int32)
    off, nbr = offsets.reshape(ENTRIES), neighbors.reshape(ENTRIES)
    far = jnp.abs(off) == 2
    key = jnp.where(far, ENTRIES, 0) + entry
    rank = jnp.sum((key[None, :] < key[:, None]).astype(jnp.int32), axis=1)
    by_b = ((off > 0) != ((x & 1) == 1)).astype(jnp.int32)
    source = jnp.where(far, by_b, jnp.where(off == 0, 1, 2 * by_b)) * BLK + nbr
    hit = (rank[None, :] == entry[:, None]).astype(jnp.int32)
    order = jnp.sum(hit * entry[None, :], axis=1)
    placed = jnp.sum(hit * source[None, :], axis=1)
    near_count = ENTRIES - jnp.sum(far.astype(jnp.int32))
    widen = lambda v: jnp.pad(v, (0, PAD - v.shape[0]))
    return widen(order), jnp.stack([widen(order // 8), widen(placed), widen(jnp.stack([near_count, x, q, x ^ col]))])


def on_device(start, blocks, neighbors, offsets, center, half_width):
    rows, width = start.shape
    col = lax.axis_index("col")
    x = lax.rem(lax.axis_index("slab"), X)
    q = lax.rem(lax.div(lax.axis_index("slab"), X), 4)
    order, meta = tables(neighbors, offsets, x, q, col)
    slab = lambda value, pairs: lax.ppermute(value, "slab", pairs)
    by_a = lambda value: slab(value, swaps(1))
    by_b = lambda value: slab(value, swaps(0))
    table = sorted_blocks(blocks.reshape(ENTRIES, BLOCK, BLOCK), order)

    def near_and_far(value, after):
        from_b = by_b(value)
        from_a = by_a(value)
        far = [by_a(from_b), by_b(from_a)]
        sources, _ = lax.optimization_barrier(([from_a, value, from_b], after))
        return near_terms(meta, table, sources), far

    def apply_operator(current, scale, others):
        result, seen = [], []
        for h in range(2):
            near, far = near_and_far(current[h], result)
            result.append(far_terms(meta, scale, table, far, near, [o[h] for o in others]))
            seen += [near, far]
        return result, seen

    inverse = 1.0 / half_width[0]
    once = jnp.stack([inverse, -center[0] * inverse])
    twice = jnp.stack([2.0 * inverse, -2.0 * center[0] * inverse, jnp.float32(-1.0)])

    grid = jnp.transpose(start.reshape(BLK, BLOCK, width), (0, 2, 1))
    previous = [grid[:, :WIDE], grid[:, WIDE:]]
    current, _ = apply_operator(previous, once, [previous])
    for level in range(2):
        previous, (current, _) = current, apply_operator(current, twice, [current, previous])
    image, seen = apply_operator(current, once, [])
    filtered = jnp.transpose(jnp.concatenate(current, axis=1), (0, 2, 1)).reshape(rows, width)

    by_col = lambda value, d: lax.ppermute(value, "col", [(c, c ^ d) for c in range(4)])
    both = jnp.stack(current)
    across = by_col(both, 2)
    both, across, _ = lax.optimization_barrier((both, across, seen))
    every = [both, by_col(both, 1), across, by_col(across, 1)]

    terms = outer(meta, every, image)
    moved = lambda d: device_pairs(lambda x, c: (x ^ d, c ^ x ^ d))
    parts = [lax.ppermute(terms[d], ("slab", "col"), moved(d)) for d in range(4)]
    beside_z = [slab_pairs(lambda y, z, x, d=d: (y, z ^ d, x)) for d in (1, 2, 3)]
    parts = small(scatter_kernel, [(2, PART, BLOCK)] * 4, meta, parts, "scatter")
    arrived = [slab(part, pairs) for part, pairs in zip(parts[1:], beside_z)]
    own = parts[0] + arrived[0] + (arrived[1] + arrived[2])
    own = own + slab(own, slab_pairs(lambda y, z, x: (y, z ^ 4, x)))
    own = own + slab(own, slab_pairs(lambda y, z, x: (y ^ 1, z, x)))
    own = own * (1.0 / (rows * SLABS))
    parts = [own] + [slab(own, pairs) for pairs in beside_z]
    (own,) = small(gather_kernel, [(2, BLOCK, BLOCK)], meta, parts, "gather")
    parts = [own] + [slab(own, slab_pairs(lambda y, z, x: (y, z, x ^ d))) for d in (1, 2, 3)]
    gram, projected = small(place_kernel, [(BLOCK, 4 * BLOCK)] * 2, meta, parts, "place")
    return filtered, gram, projected


def solution(mesh):
    return jax.shard_map(
        on_device,
        mesh=mesh,
        in_specs=(
            P("slab", "col"),
            P("slab", None, None, None),
            P("slab", None),
            P("slab", None),
            P(),
            P(),
        ),
        out_specs=(P("slab", "col"), P("col", None), P("col", None)),
        check_vma=False,
    )
```

```python
import functools

import jax
import jax.numpy as jnp
from jax import lax
from jax.experimental import pallas as pl
from jax.experimental.pallas import tpu as pltpu
from jax.sharding import PartitionSpec as P

BLOCK = 128
BLK = 16
WIDE = 64
ENTRIES = 128
GROUP = 16
SORTED = 16
PAD = ENTRIES + SORTED
YH, Z, X = 2, 8, 4
SLABS = YH * Z * X


def slab_of(y, z, x):
    return (y * Z + z) * X + x


def swaps(first):
    pairs = []
    for s in range(first, SLABS, 2):
        t = (s + 1) % SLABS
        pairs += [(s, t), (t, s)]
    return pairs


def slab_pairs(target):
    return [(slab_of(y, z, x), slab_of(*target(y, z, x))) for y in range(YH) for z in range(Z) for x in range(X)]


def device_pairs(target):
    pairs = []
    for s in range(SLABS):
        y, z, x = s // (Z * X), s // X % Z, s % X
        for c in range(4):
            to_x, to_c = target(x, c)
            pairs.append((s * 4 + c, slab_of(y, z, to_x) * 4 + to_c))
    return pairs


def split(value):
    high = value.astype(jnp.bfloat16)
    return high, (value - high.astype(jnp.float32)).astype(jnp.bfloat16)


def across_lanes(a, b):
    return lax.dot_general(a, b, (((1,), (1,)), ((), ())), preferred_element_type=jnp.float32)


ANY = pl.BlockSpec(memory_space=pl.ANY)
SMEM = pl.BlockSpec(memory_space=pltpu.SMEM)
VMEM = pl.BlockSpec(memory_space=pltpu.VMEM)


def sort_kernel(order, *refs):
    out = refs[-1]
    for u in range(SORTED):
        high, low = split(refs[u][0])
        out[u, :, :BLOCK] = high
        out[u, :, BLOCK:] = low


def sorted_blocks(blocks, order):
    spec = lambda u: pl.BlockSpec((1, BLOCK, BLOCK), lambda g, order: (order[g * SORTED + u], 0, 0))
    return pl.pallas_call(
        sort_kernel,
        out_shape=jax.ShapeDtypeStruct((PAD, BLOCK, 2 * BLOCK), jnp.bfloat16),
        grid_spec=pltpu.PrefetchScalarGridSpec(
            num_scalar_prefetch=1,
            grid=(PAD // SORTED,),
            in_specs=[spec(u) for u in range(SORTED)],
            out_specs=pl.BlockSpec((SORTED, BLOCK, 2 * BLOCK), lambda g, order: (g, 0, 0)),
        ),
        compiler_params=pltpu.CompilerParams(vmem_limit_bytes=16 << 20),
        cost_estimate=pl.CostEstimate(flops=0, bytes_accessed=24 << 20, transcendentals=0),
        name="sort_blocks",
    )(order, *[blocks] * SORTED)


def accumulate(meta, table, sources, held, sems, acc, first, last):
    loads = []
    for j, source in enumerate(sources):
        loads.append(pltpu.make_async_copy(source, held.at[pl.ds(j * BLK, BLK)], sems.at[j]))
        loads[-1].start()
    for load in loads:
        load.wait()

    def step(k, carry):
        terms, rows = [], []
        for u in range(GROUP):
            e = first + k * GROUP + u
            value = held[meta[1, e]]
            high, low = split(jnp.where(e < last, value, jnp.zeros_like(value)))
            lhs = jnp.concatenate(
                [jnp.concatenate([high, high], axis=1), jnp.concatenate([low, jnp.zeros_like(low)], axis=1)], axis=0
            )
            both = across_lanes(lhs, table[e])
            terms.append(both[:WIDE] + both[WIDE:])
            rows.append(meta[0, e])
        for u in range(GROUP):
            acc[rows[u]] += terms[u]
        return carry

    lax.fori_loop(0, lax.div(last - first + (GROUP - 1), GROUP), step, 0)


HELD = (BLK, WIDE, BLOCK)


def scratch(slabs):
    return [
        pltpu.VMEM((slabs * BLK, WIDE, BLOCK), jnp.float32),
        pltpu.SemaphoreType.DMA((slabs,)),
    ]


def cost(entries):
    return pl.CostEstimate(flops=entries * 6 * BLOCK**3, bytes_accessed=entries * 4 * BLOCK**2, transcendentals=0)


def near_kernel(meta, table, *refs):
    sources, (acc, held, sems) = refs[:3], refs[3:]
    acc[...] = jnp.zeros_like(acc)
    accumulate(meta, table, sources, held, sems, acc, 0, meta[2, 0])


def near_terms(meta, table, sources):
    return pl.pallas_call(
        near_kernel,
        out_shape=jax.ShapeDtypeStruct(HELD, jnp.float32),
        in_specs=[SMEM, VMEM] + [ANY] * 3,
        out_specs=VMEM,
        scratch_shapes=scratch(3),
        compiler_params=pltpu.CompilerParams(vmem_limit_bytes=16 << 20),
        cost_estimate=cost(80),
        name="near_terms",
    )(meta, table, *sources)


def far_kernel(parts, meta, scale, table, *refs):
    sources, near, others, (out, held, sems) = refs[:2], refs[2], refs[3 : 3 + parts], refs[3 + parts :]
    out[...] = near[...]
    accumulate(meta, table, sources, held, sems, out, meta[2, 0], ENTRIES)
    if parts:
        value = out[...] * scale[0]
        for j in range(parts):
            value = value + others[j][...] * scale[j + 1]
        out[...] = value


def far_terms(meta, scale, table, sources, near, others):
    return pl.pallas_call(
        functools.partial(far_kernel, len(others)),
        out_shape=jax.ShapeDtypeStruct(HELD, jnp.float32),
        in_specs=[SMEM, SMEM, VMEM] + [ANY] * 2 + [VMEM] * (1 + len(others)),
        out_specs=VMEM,
        scratch_shapes=scratch(2),
        compiler_params=pltpu.CompilerParams(vmem_limit_bytes=16 << 20),
        cost_estimate=cost(52),
        name="far_terms",
    )(meta, scale, table, *sources, near, *others)


def outer_kernel(meta, *refs):
    every, outs, total = refs[:8], refs[10:14], refs[14]
    right = every[:2] + refs[8:10]
    total[...] = jnp.zeros_like(total)

    def step(k, carry):
        def some(ref):
            return jnp.concatenate([ref[4 * k + i] for i in range(4)], axis=-1)

        a = split(jnp.concatenate([some(ref) for ref in every], axis=0))
        b = split(jnp.concatenate([some(ref) for ref in right], axis=0))
        total[...] += across_lanes(a[0], b[0]) + (across_lanes(a[0], b[1]) + across_lanes(a[1], b[0]))
        return carry

    lax.fori_loop(0, BLK // 4, step, 0)
    for d in range(4):
        part = pl.ds(pl.multiple_of((meta[2, 1] ^ d) * BLOCK, BLOCK), BLOCK)
        for k in range(2):
            outs[d][k] = total[part, k * BLOCK : (k + 1) * BLOCK]


def outer(meta, every, image):
    return pl.pallas_call(
        outer_kernel,
        out_shape=[jax.ShapeDtypeStruct((2, BLOCK, BLOCK), jnp.float32)] * 4,
        in_specs=[SMEM] + [VMEM] * 10,
        out_specs=[VMEM] * 4,
        scratch_shapes=[pltpu.VMEM((4 * BLOCK, 2 * BLOCK), jnp.float32)],
        compiler_params=pltpu.CompilerParams(vmem_limit_bytes=12 << 20),
        cost_estimate=pl.CostEstimate(flops=6 * 2048 * 512 * 256, bytes_accessed=6 << 20, transcendentals=0),
        name="outer",
    )(meta, *every, *image)


PART = BLOCK // 4


def small(kernel, outs, meta, parts, name):
    return pl.pallas_call(
        kernel,
        out_shape=[jax.ShapeDtypeStruct(shape, jnp.float32) for shape in outs],
        in_specs=[SMEM] + [VMEM] * len(parts),
        out_specs=[VMEM] * len(outs),
        compiler_params=pltpu.CompilerParams(vmem_limit_bytes=4 << 20),
        name=name,
    )(meta, *parts)


def quarter(meta, d):
    return pl.ds(pl.multiple_of((meta[2, 2] ^ d) * PART, PART), PART)


def scatter_kernel(meta, *refs):
    for d in range(4):
        part = quarter(meta, d)
        for k in range(2):
            refs[4 + d][k] = (refs[0][k, part] + refs[1][k, part]) + (refs[2][k, part] + refs[3][k, part])


def gather_kernel(meta, *refs):
    for d in range(4):
        for k in range(2):
            refs[4][k, quarter(meta, d)] = refs[d][k]


def place_kernel(meta, *refs):
    for d in range(4):
        columns = pl.ds(pl.multiple_of((meta[2, 3] ^ d) * BLOCK, BLOCK), BLOCK)
        for k in range(2):
            refs[4 + k][:, columns] = refs[d][k]


def tables(neighbors, offsets, x, q, col):
    entry = jnp.arange(ENTRIES, dtype=jnp.int32)
    off, nbr = offsets.reshape(ENTRIES), neighbors.reshape(ENTRIES)
    far = jnp.abs(off) == 2
    key = jnp.where(far, ENTRIES, 0) + entry
    rank = jnp.sum((key[None, :] < key[:, None]).astype(jnp.int32), axis=1)
    by_b = ((off > 0) != ((x & 1) == 1)).astype(jnp.int32)
    source = jnp.where(far, by_b, jnp.where(off == 0, 1, 2 * by_b)) * BLK + nbr
    hit = (rank[None, :] == entry[:, None]).astype(jnp.int32)
    order = jnp.sum(hit * entry[None, :], axis=1)
    placed = jnp.sum(hit * source[None, :], axis=1)
    near_count = ENTRIES - jnp.sum(far.astype(jnp.int32))
    widen = lambda v: jnp.pad(v, (0, PAD - v.shape[0]))
    return widen(order), jnp.stack([widen(order // 8), widen(placed), widen(jnp.stack([near_count, x, q, x ^ col]))])


def on_device(start, blocks, neighbors, offsets, center, half_width):
    rows, width = start.shape
    col = lax.axis_index("col")
    x = lax.rem(lax.axis_index("slab"), X)
    q = lax.rem(lax.div(lax.axis_index("slab"), X), 4)
    order, meta = tables(neighbors, offsets, x, q, col)
    slab = lambda value, pairs: lax.ppermute(value, "slab", pairs)
    by_a = lambda value: slab(value, swaps(1))
    by_b = lambda value: slab(value, swaps(0))
    table = sorted_blocks(blocks.reshape(ENTRIES, BLOCK, BLOCK), order)

    def near_and_far(value, after):
        from_b = by_b(value)
        from_a = by_a(value)
        far = [by_a(from_b), by_b(from_a)]
        sources, _ = lax.optimization_barrier(([from_a, value, from_b], after))
        return near_terms(meta, table, sources), far

    def apply_operator(current, scale, others, first=()):
        result, seen = [], []
        for h in range(2):
            near, far = near_and_far(current[h], result or list(first))
            result.append(far_terms(meta, scale, table, far, near, [o[h] for o in others]))
            seen += [near, far]
        return result, seen

    inverse = 1.0 / half_width[0]
    once = jnp.stack([inverse, -center[0] * inverse])
    twice = jnp.stack([2.0 * inverse, -2.0 * center[0] * inverse, jnp.float32(-1.0)])

    grid = jnp.transpose(start.reshape(BLK, BLOCK, width), (0, 2, 1))
    previous = [grid[:, :WIDE], grid[:, WIDE:]]
    current, _ = apply_operator(previous, once, [previous])
    for level in range(2):
        previous, (current, _) = current, apply_operator(current, twice, [current, previous])
    by_col = lambda value, d: lax.ppermute(value, "col", [(c, c ^ d) for c in range(4)])
    early = by_col(current[0], 2)
    image, seen = apply_operator(current, once, [], [early])
    filtered = jnp.transpose(jnp.concatenate(current, axis=1), (0, 2, 1)).reshape(rows, width)

    later, _ = lax.optimization_barrier((current[1], seen[:2]))
    across = [early, by_col(later, 2)]
    ready, _ = lax.optimization_barrier((current + across[:1], seen))
    beside = [by_col(h, 1) for h in ready[:2]]
    diagonal = [by_col(ready[2], 1), by_col(across[1], 1)]
    every = current + beside + across + diagonal

    terms = outer(meta, every, image)
    moved = lambda d: device_pairs(lambda x, c: (x ^ d, c ^ x ^ d))
    parts = [lax.ppermute(terms[d], ("slab", "col"), moved(d)) for d in range(4)]
    beside_z = [slab_pairs(lambda y, z, x, d=d: (y, z ^ d, x)) for d in (1, 2, 3)]
    parts = small(scatter_kernel, [(2, PART, BLOCK)] * 4, meta, parts, "scatter")
    arrived = [slab(part, pairs) for part, pairs in zip(parts[1:], beside_z)]
    own = parts[0] + arrived[0] + (arrived[1] + arrived[2])
    own = own + slab(own, slab_pairs(lambda y, z, x: (y, z ^ 4, x)))
    own = own + slab(own, slab_pairs(lambda y, z, x: (y ^ 1, z, x)))
    own = own * (1.0 / (rows * SLABS))
    parts = [own] + [slab(own, pairs) for pairs in beside_z]
    (own,) = small(gather_kernel, [(2, BLOCK, BLOCK)], meta, parts, "gather")
    parts = [own] + [slab(own, slab_pairs(lambda y, z, x: (y, z, x ^ d))) for d in (1, 2, 3)]
    gram, projected = small(place_kernel, [(BLOCK, 4 * BLOCK)] * 2, meta, parts, "place")
    return filtered, gram, projected


def solution(mesh):
    return jax.shard_map(
        on_device,
        mesh=mesh,
        in_specs=(
            P("slab", "col"),
            P("slab", None, None, None),
            P("slab", None),
            P("slab", None),
            P(),
            P(),
        ),
        out_specs=(P("slab", "col"), P("col", None), P("col", None)),
        check_vma=False,
    )
```

```python
import functools

import jax
import jax.numpy as jnp
from jax import lax
from jax.experimental import pallas as pl
from jax.experimental.pallas import tpu as pltpu
from jax.sharding import PartitionSpec as P

BLOCK = 128
BLK = 16
WIDE = 64
ENTRIES = 128
GROUP = 16
SORTED = 16
PAD = ENTRIES + SORTED
YH, Z, X = 2, 8, 4
SLABS = YH * Z * X


def slab_of(y, z, x):
    return (y * Z + z) * X + x


def swaps(first):
    pairs = []
    for s in range(first, SLABS, 2):
        t = (s + 1) % SLABS
        pairs += [(s, t), (t, s)]
    return pairs


def slab_pairs(target):
    return [(slab_of(y, z, x), slab_of(*target(y, z, x))) for y in range(YH) for z in range(Z) for x in range(X)]


def device_pairs(target):
    pairs = []
    for s in range(SLABS):
        y, z, x = s // (Z * X), s // X % Z, s % X
        for c in range(4):
            to_x, to_c = target(x, c)
            pairs.append((s * 4 + c, slab_of(y, z, to_x) * 4 + to_c))
    return pairs


def split(value):
    high = value.astype(jnp.bfloat16)
    return high, (value - high.astype(jnp.float32)).astype(jnp.bfloat16)


def across_lanes(a, b):
    return lax.dot_general(a, b, (((1,), (1,)), ((), ())), preferred_element_type=jnp.float32)


ANY = pl.BlockSpec(memory_space=pl.ANY)
SMEM = pl.BlockSpec(memory_space=pltpu.SMEM)
VMEM = pl.BlockSpec(memory_space=pltpu.VMEM)


def sort_kernel(order, *refs):
    out = refs[-1]
    for u in range(SORTED):
        high, low = split(refs[u][0])
        out[u, :, :BLOCK] = high
        out[u, :, BLOCK:] = low


def sorted_blocks(blocks, order):
    spec = lambda u: pl.BlockSpec((1, BLOCK, BLOCK), lambda g, order: (order[g * SORTED + u], 0, 0))
    return pl.pallas_call(
        sort_kernel,
        out_shape=jax.ShapeDtypeStruct((PAD, BLOCK, 2 * BLOCK), jnp.bfloat16),
        grid_spec=pltpu.PrefetchScalarGridSpec(
            num_scalar_prefetch=1,
            grid=(PAD // SORTED,),
            in_specs=[spec(u) for u in range(SORTED)],
            out_specs=pl.BlockSpec((SORTED, BLOCK, 2 * BLOCK), lambda g, order: (g, 0, 0)),
        ),
        compiler_params=pltpu.CompilerParams(vmem_limit_bytes=16 << 20),
        cost_estimate=pl.CostEstimate(flops=0, bytes_accessed=24 << 20, transcendentals=0),
        name="sort_blocks",
    )(order, *[blocks] * SORTED)


def accumulate(meta, table, sources, held, sems, acc, first, last):
    loads = []
    for j, source in enumerate(sources):
        loads.append(pltpu.make_async_copy(source, held.at[pl.ds(j * BLK, BLK)], sems.at[j]))
        loads[-1].start()
    for load in loads:
        load.wait()

    def step(k, carry):
        terms, rows = [], []
        for u in range(GROUP):
            e = first + k * GROUP + u
            value = held[meta[1, e]]
            high, low = split(jnp.where(e < last, value, jnp.zeros_like(value)))
            lhs = jnp.concatenate(
                [jnp.concatenate([high, high], axis=1), jnp.concatenate([low, jnp.zeros_like(low)], axis=1)], axis=0
            )
            both = across_lanes(lhs, table[e])
            terms.append(both[:WIDE] + both[WIDE:])
            rows.append(meta[0, e])
        for u in range(GROUP):
            acc[rows[u]] += terms[u]
        return carry

    lax.fori_loop(0, lax.div(last - first + (GROUP - 1), GROUP), step, 0)


HELD = (BLK, WIDE, BLOCK)


def scratch(slabs):
    return [
        pltpu.VMEM((slabs * BLK, WIDE, BLOCK), jnp.float32),
        pltpu.SemaphoreType.DMA((slabs,)),
    ]


def cost(entries):
    return pl.CostEstimate(flops=entries * 6 * BLOCK**3, bytes_accessed=entries * 4 * BLOCK**2, transcendentals=0)


def near_kernel(meta, table, *refs):
    sources, (acc, held, sems) = refs[:3], refs[3:]
    acc[...] = jnp.zeros_like(acc)
    accumulate(meta, table, sources, held, sems, acc, 0, meta[2, 0])


def near_terms(meta, table, sources):
    return pl.pallas_call(
        near_kernel,
        out_shape=jax.ShapeDtypeStruct(HELD, jnp.float32),
        in_specs=[SMEM, VMEM] + [ANY] * 3,
        out_specs=VMEM,
        scratch_shapes=scratch(3),
        compiler_params=pltpu.CompilerParams(vmem_limit_bytes=16 << 20),
        cost_estimate=cost(80),
        name="near_terms",
    )(meta, table, *sources)


def far_kernel(parts, meta, scale, table, *refs):
    sources, near, others, (out, held, sems) = refs[:2], refs[2], refs[3 : 3 + parts], refs[3 + parts :]
    out[...] = near[...]
    accumulate(meta, table, sources, held, sems, out, meta[2, 0], ENTRIES)
    if parts:
        value = out[...] * scale[0]
        for j in range(parts):
            value = value + others[j][...] * scale[j + 1]
        out[...] = value


def far_terms(meta, scale, table, sources, near, others):
    return pl.pallas_call(
        functools.partial(far_kernel, len(others)),
        out_shape=jax.ShapeDtypeStruct(HELD, jnp.float32),
        in_specs=[SMEM, SMEM, VMEM] + [ANY] * 2 + [VMEM] * (1 + len(others)),
        out_specs=VMEM,
        scratch_shapes=scratch(2),
        compiler_params=pltpu.CompilerParams(vmem_limit_bytes=16 << 20),
        cost_estimate=cost(52),
        name="far_terms",
    )(meta, scale, table, *sources, near, *others)


def products(columns, right, total):
    total[...] = jnp.zeros_like(total)

    def step(k, carry):
        def some(ref):
            return jnp.concatenate([ref[4 * k + i] for i in range(4)], axis=-1)

        a = split(jnp.concatenate([some(ref) for ref in columns], axis=0))
        b = split(jnp.concatenate([some(ref) for ref in right], axis=0))
        total[...] += across_lanes(a[0], b[0]) + (across_lanes(a[0], b[1]) + across_lanes(a[1], b[0]))
        return carry

    lax.fori_loop(0, BLK // 4, step, 0)


def halves(refs):
    return [ref.at[h] for ref in refs for h in range(2)]


def near_outer_kernel(*refs):
    columns = halves(refs[:2])
    products(columns, columns[:2] + list(refs[2:4]), refs[4])


def outer_kernel(meta, *refs):
    right, outs, total = halves(refs[:1]) + list(refs[3:5]), refs[6:10], refs[10]
    products(halves(refs[1:3]), right, total.at[2 * BLOCK :])
    total[: 2 * BLOCK] = refs[5][...]
    for d in range(4):
        part = pl.ds(pl.multiple_of((meta[2, 1] ^ d) * BLOCK, BLOCK), BLOCK)
        for k in range(2):
            outs[d][k] = total[part, k * BLOCK : (k + 1) * BLOCK]


def near_outer(every, image):
    return pl.pallas_call(
        near_outer_kernel,
        out_shape=jax.ShapeDtypeStruct((2 * BLOCK, 2 * BLOCK), jnp.float32),
        in_specs=[VMEM] * 4,
        out_specs=VMEM,
        compiler_params=pltpu.CompilerParams(vmem_limit_bytes=12 << 20),
        cost_estimate=pl.CostEstimate(flops=6 * 2048 * 256 * 256, bytes_accessed=4 << 20, transcendentals=0),
        name="near_outer",
    )(*every, *image)


def outer(meta, both, every, image, near):
    return pl.pallas_call(
        outer_kernel,
        out_shape=[jax.ShapeDtypeStruct((2, BLOCK, BLOCK), jnp.float32)] * 4,
        in_specs=[SMEM] + [VMEM] * 6,
        out_specs=[VMEM] * 4,
        scratch_shapes=[pltpu.VMEM((4 * BLOCK, 2 * BLOCK), jnp.float32)],
        compiler_params=pltpu.CompilerParams(vmem_limit_bytes=12 << 20),
        cost_estimate=pl.CostEstimate(flops=6 * 2048 * 256 * 256, bytes_accessed=4 << 20, transcendentals=0),
        name="outer",
    )(meta, both, *every, *image, near)


PART = BLOCK // 4


def small(kernel, outs, meta, parts, name):
    return pl.pallas_call(
        kernel,
        out_shape=[jax.ShapeDtypeStruct(shape, jnp.float32) for shape in outs],
        in_specs=[SMEM] + [VMEM] * len(parts),
        out_specs=[VMEM] * len(outs),
        compiler_params=pltpu.CompilerParams(vmem_limit_bytes=4 << 20),
        name=name,
    )(meta, *parts)


def quarter(meta, d):
    return pl.ds(pl.multiple_of((meta[2, 2] ^ d) * PART, PART), PART)


def scatter_kernel(meta, *refs):
    for d in range(4):
        part = quarter(meta, d)
        for k in range(2):
            refs[4 + d][k] = (refs[0][k, part] + refs[1][k, part]) + (refs[2][k, part] + refs[3][k, part])


def gather_kernel(meta, *refs):
    for d in range(4):
        for k in range(2):
            refs[4][k, quarter(meta, d)] = refs[d][k]


def place_kernel(meta, *refs):
    for d in range(4):
        columns = pl.ds(pl.multiple_of((meta[2, 3] ^ d) * BLOCK, BLOCK), BLOCK)
        for k in range(2):
            refs[4 + k][:, columns] = refs[d][k]


def tables(neighbors, offsets, x, q, col):
    entry = jnp.arange(ENTRIES, dtype=jnp.int32)
    off, nbr = offsets.reshape(ENTRIES), neighbors.reshape(ENTRIES)
    far = jnp.abs(off) == 2
    key = jnp.where(far, ENTRIES, 0) + entry
    rank = jnp.sum((key[None, :] < key[:, None]).astype(jnp.int32), axis=1)
    by_b = ((off > 0) != ((x & 1) == 1)).astype(jnp.int32)
    source = jnp.where(far, by_b, jnp.where(off == 0, 1, 2 * by_b)) * BLK + nbr
    hit = (rank[None, :] == entry[:, None]).astype(jnp.int32)
    order = jnp.sum(hit * entry[None, :], axis=1)
    placed = jnp.sum(hit * source[None, :], axis=1)
    near_count = ENTRIES - jnp.sum(far.astype(jnp.int32))
    widen = lambda v: jnp.pad(v, (0, PAD - v.shape[0]))
    return widen(order), jnp.stack([widen(order // 8), widen(placed), widen(jnp.stack([near_count, x, q, x ^ col]))])


def on_device(start, blocks, neighbors, offsets, center, half_width):
    rows, width = start.shape
    col = lax.axis_index("col")
    x = lax.rem(lax.axis_index("slab"), X)
    q = lax.rem(lax.div(lax.axis_index("slab"), X), 4)
    order, meta = tables(neighbors, offsets, x, q, col)
    slab = lambda value, pairs: lax.ppermute(value, "slab", pairs)
    by_a = lambda value: slab(value, swaps(1))
    by_b = lambda value: slab(value, swaps(0))
    table = sorted_blocks(blocks.reshape(ENTRIES, BLOCK, BLOCK), order)

    def near_and_far(value, after, start_after=()):
        value, _ = lax.optimization_barrier((value, list(start_after)))
        from_b = by_b(value)
        from_a = by_a(value)
        far = [by_a(from_b), by_b(from_a)]
        sources, _ = lax.optimization_barrier(([from_a, value, from_b], after))
        return near_terms(meta, table, sources), far, from_b

    def apply_operator(current, scale, others, staggered=False):
        result, seen, arrived = [], [], []
        for h in range(2):
            near, far, from_b = near_and_far(current[h], result, arrived)
            arrived = [from_b] if staggered else []
            result.append(far_terms(meta, scale, table, far, near, [o[h] for o in others]))
            seen += [near, far]
        return result, seen

    inverse = 1.0 / half_width[0]
    once = jnp.stack([inverse, -center[0] * inverse])
    twice = jnp.stack([2.0 * inverse, -2.0 * center[0] * inverse, jnp.float32(-1.0)])

    grid = jnp.transpose(start.reshape(BLK, BLOCK, width), (0, 2, 1))
    previous = [grid[:, :WIDE], grid[:, WIDE:]]
    current, _ = apply_operator(previous, once, [previous], True)
    for level in range(2):
        previous, (current, _) = current, apply_operator(current, twice, [current, previous])
    image, seen = apply_operator(current, once, [])
    filtered = jnp.transpose(jnp.concatenate(current, axis=1), (0, 2, 1)).reshape(rows, width)

    by_col = lambda value, d: lax.ppermute(value, "col", [(c, c ^ d) for c in range(4)])
    both = jnp.stack(current)
    across = by_col(both, 2)
    ready, _ = lax.optimization_barrier((both, seen))
    first = near_outer([both, by_col(ready, 1)], image)
    across, first = lax.optimization_barrier((across, first))

    terms = outer(meta, both, [across, by_col(across, 1)], image, first)
    moved = lambda d: device_pairs(lambda x, c: (x ^ d, c ^ x ^ d))
    parts = [lax.ppermute(terms[d], ("slab", "col"), moved(d)) for d in range(4)]
    beside_z = [slab_pairs(lambda y, z, x, d=d: (y, z ^ d, x)) for d in (1, 2, 3)]
    parts = small(scatter_kernel, [(2, PART, BLOCK)] * 4, meta, parts, "scatter")
    arrived = [slab(part, pairs) for part, pairs in zip(parts[1:], beside_z)]
    own = parts[0] + arrived[0] + (arrived[1] + arrived[2])
    own = own + slab(own, slab_pairs(lambda y, z, x: (y, z ^ 4, x)))
    own = own + slab(own, slab_pairs(lambda y, z, x: (y ^ 1, z, x)))
    own = own * (1.0 / (rows * SLABS))
    parts = [own] + [slab(own, pairs) for pairs in beside_z]
    (own,) = small(gather_kernel, [(2, BLOCK, BLOCK)], meta, parts, "gather")
    parts = [own] + [slab(own, slab_pairs(lambda y, z, x: (y, z, x ^ d))) for d in (1, 2, 3)]
    gram, projected = small(place_kernel, [(BLOCK, 4 * BLOCK)] * 2, meta, parts, "place")
    return filtered, gram, projected


def solution(mesh):
    return jax.shard_map(
        on_device,
        mesh=mesh,
        in_specs=(
            P("slab", "col"),
            P("slab", None, None, None),
            P("slab", None),
            P("slab", None),
            P(),
            P(),
        ),
        out_specs=(P("slab", "col"), P("col", None), P("col", None)),
        check_vma=False,
    )
```

```python
import functools

import jax
import jax.numpy as jnp
from jax import lax
from jax.experimental import pallas as pl
from jax.experimental.pallas import tpu as pltpu
from jax.sharding import PartitionSpec as P

BLOCK = 128
BLK = 16
WIDE = 64
ENTRIES = 128
GROUP = 16
SORTED = 16
PAD = ENTRIES + SORTED
YH, Z, X = 2, 8, 4
SLABS = YH * Z * X
AT_WRAP = [(0, 1), (31, 30), (32, 33), (63, 62)]


def slab_of(y, z, x):
    return (y * Z + z) * X + x


def swaps(first):
    pairs = []
    for s in range(first, SLABS, 2):
        t = (s + 1) % SLABS
        pairs += [(s, t), (t, s)]
    return pairs


def slab_pairs(target):
    return [(slab_of(y, z, x), slab_of(*target(y, z, x))) for y in range(YH) for z in range(Z) for x in range(X)]


def device_pairs(target):
    pairs = []
    for s in range(SLABS):
        y, z, x = s // (Z * X), s // X % Z, s % X
        for c in range(4):
            to_x, to_c = target(x, c)
            pairs.append((s * 4 + c, slab_of(y, z, to_x) * 4 + to_c))
    return pairs


def split(value):
    high = value.astype(jnp.bfloat16)
    return high, (value - high.astype(jnp.float32)).astype(jnp.bfloat16)


def across_lanes(a, b):
    return lax.dot_general(a, b, (((1,), (1,)), ((), ())), preferred_element_type=jnp.float32)


ANY = pl.BlockSpec(memory_space=pl.ANY)
SMEM = pl.BlockSpec(memory_space=pltpu.SMEM)
VMEM = pl.BlockSpec(memory_space=pltpu.VMEM)


def sort_kernel(order, *refs):
    out = refs[-1]
    for u in range(SORTED):
        high, low = split(refs[u][0])
        out[u, :, :BLOCK] = high
        out[u, :, BLOCK:] = low


def sorted_blocks(blocks, order):
    spec = lambda u: pl.BlockSpec((1, BLOCK, BLOCK), lambda g, order: (order[g * SORTED + u], 0, 0))
    return pl.pallas_call(
        sort_kernel,
        out_shape=jax.ShapeDtypeStruct((PAD, BLOCK, 2 * BLOCK), jnp.bfloat16),
        grid_spec=pltpu.PrefetchScalarGridSpec(
            num_scalar_prefetch=1,
            grid=(PAD // SORTED,),
            in_specs=[spec(u) for u in range(SORTED)],
            out_specs=pl.BlockSpec((SORTED, BLOCK, 2 * BLOCK), lambda g, order: (g, 0, 0)),
        ),
        compiler_params=pltpu.CompilerParams(vmem_limit_bytes=16 << 20),
        cost_estimate=pl.CostEstimate(flops=0, bytes_accessed=24 << 20, transcendentals=0),
        name="sort_blocks",
    )(order, *[blocks] * SORTED)


def accumulate(meta, table, sources, held, sems, acc, first, last):
    loads = []
    for j, source in enumerate(sources):
        loads.append(pltpu.make_async_copy(source, held.at[pl.ds(j * BLK, BLK)], sems.at[j]))
        loads[-1].start()
    for load in loads:
        load.wait()

    def step(k, carry):
        terms, rows = [], []
        for u in range(GROUP):
            e = first + k * GROUP + u
            value = held[meta[1, e]]
            high, low = split(jnp.where(e < last, value, jnp.zeros_like(value)))
            lhs = jnp.concatenate(
                [jnp.concatenate([high, high], axis=1), jnp.concatenate([low, jnp.zeros_like(low)], axis=1)], axis=0
            )
            both = across_lanes(lhs, table[e])
            terms.append(both[:WIDE] + both[WIDE:])
            rows.append(meta[0, e])
        for u in range(GROUP):
            acc[rows[u]] += terms[u]
        return carry

    lax.fori_loop(0, lax.div(last - first + (GROUP - 1), GROUP), step, 0)


HELD = (BLK, WIDE, BLOCK)


def scratch(slabs):
    return [
        pltpu.VMEM((slabs * BLK, WIDE, BLOCK), jnp.float32),
        pltpu.SemaphoreType.DMA((slabs,)),
    ]


def cost(entries):
    return pl.CostEstimate(flops=entries * 6 * BLOCK**3, bytes_accessed=entries * 4 * BLOCK**2, transcendentals=0)


def near_kernel(meta, table, *refs):
    sources, (acc, held, sems) = refs[:3], refs[3:]
    acc[...] = jnp.zeros_like(acc)
    accumulate(meta, table, sources, held, sems, acc, 0, meta[2, 0])


def near_terms(meta, table, sources):
    return pl.pallas_call(
        near_kernel,
        out_shape=jax.ShapeDtypeStruct(HELD, jnp.float32),
        in_specs=[SMEM, VMEM] + [ANY] * 3,
        out_specs=VMEM,
        scratch_shapes=scratch(3),
        compiler_params=pltpu.CompilerParams(vmem_limit_bytes=16 << 20),
        cost_estimate=cost(80),
        name="near_terms",
    )(meta, table, *sources)


def far_kernel(parts, meta, scale, table, *refs):
    sources, near, others, (out, held, sems) = refs[:2], refs[2], refs[3 : 3 + parts], refs[3 + parts :]
    out[...] = near[...]
    accumulate(meta, table, sources, held, sems, out, meta[2, 0], ENTRIES)
    if parts:
        value = out[...] * scale[0]
        for j in range(parts):
            value = value + others[j][...] * scale[j + 1]
        out[...] = value


def far_terms(meta, scale, table, sources, near, others):
    return pl.pallas_call(
        functools.partial(far_kernel, len(others)),
        out_shape=jax.ShapeDtypeStruct(HELD, jnp.float32),
        in_specs=[SMEM, SMEM, VMEM] + [ANY] * 2 + [VMEM] * (1 + len(others)),
        out_specs=VMEM,
        scratch_shapes=scratch(2),
        compiler_params=pltpu.CompilerParams(vmem_limit_bytes=16 << 20),
        cost_estimate=cost(52),
        name="far_terms",
    )(meta, scale, table, *sources, near, *others)


def outer_kernel(meta, *refs):
    every, outs, total = refs[:8], refs[10:14], refs[14]
    right = every[:2] + refs[8:10]
    total[...] = jnp.zeros_like(total)

    def step(k, carry):
        def some(ref):
            return jnp.concatenate([ref[4 * k + i] for i in range(4)], axis=-1)

        a = split(jnp.concatenate([some(ref) for ref in every], axis=0))
        b = split(jnp.concatenate([some(ref) for ref in right], axis=0))
        total[...] += across_lanes(a[0], b[0]) + (across_lanes(a[0], b[1]) + across_lanes(a[1], b[0]))
        return carry

    lax.fori_loop(0, BLK // 4, step, 0)
    for d in range(4):
        part = pl.ds(pl.multiple_of((meta[2, 1] ^ d) * BLOCK, BLOCK), BLOCK)
        for k in range(2):
            outs[d][k] = total[part, k * BLOCK : (k + 1) * BLOCK]


def outer(meta, every, image):
    return pl.pallas_call(
        outer_kernel,
        out_shape=[jax.ShapeDtypeStruct((2, BLOCK, BLOCK), jnp.float32)] * 4,
        in_specs=[SMEM] + [VMEM] * 10,
        out_specs=[VMEM] * 4,
        scratch_shapes=[pltpu.VMEM((4 * BLOCK, 2 * BLOCK), jnp.float32)],
        compiler_params=pltpu.CompilerParams(vmem_limit_bytes=12 << 20),
        cost_estimate=pl.CostEstimate(flops=6 * 2048 * 512 * 256, bytes_accessed=6 << 20, transcendentals=0),
        name="outer",
    )(meta, *every, *image)


PART = BLOCK // 4


def small(kernel, outs, meta, parts, name):
    return pl.pallas_call(
        kernel,
        out_shape=[jax.ShapeDtypeStruct(shape, jnp.float32) for shape in outs],
        in_specs=[SMEM] + [VMEM] * len(parts),
        out_specs=[VMEM] * len(outs),
        compiler_params=pltpu.CompilerParams(vmem_limit_bytes=4 << 20),
        name=name,
    )(meta, *parts)


def quarter(meta, d):
    return pl.ds(pl.multiple_of((meta[2, 2] ^ d) * PART, PART), PART)


def scatter_kernel(meta, *refs):
    for d in range(4):
        part = quarter(meta, d)
        for k in range(2):
            refs[4 + d][k] = (refs[0][k, part] + refs[1][k, part]) + (refs[2][k, part] + refs[3][k, part])


def gather_kernel(meta, *refs):
    for d in range(4):
        for k in range(2):
            refs[4][k, quarter(meta, d)] = refs[d][k]


def place_kernel(meta, *refs):
    for d in range(4):
        columns = pl.ds(pl.multiple_of((meta[2, 3] ^ d) * BLOCK, BLOCK), BLOCK)
        for k in range(2):
            refs[4 + k][:, columns] = refs[d][k]


def tables(neighbors, offsets, x, q, col):
    entry = jnp.arange(ENTRIES, dtype=jnp.int32)
    off, nbr = offsets.reshape(ENTRIES), neighbors.reshape(ENTRIES)
    far = jnp.abs(off) == 2
    key = jnp.where(far, ENTRIES, 0) + entry
    rank = jnp.sum((key[None, :] < key[:, None]).astype(jnp.int32), axis=1)
    by_b = ((off > 0) != ((x & 1) == 1)).astype(jnp.int32)
    source = jnp.where(far, by_b, jnp.where(off == 0, 1, 2 * by_b)) * BLK + nbr
    hit = (rank[None, :] == entry[:, None]).astype(jnp.int32)
    order = jnp.sum(hit * entry[None, :], axis=1)
    placed = jnp.sum(hit * source[None, :], axis=1)
    near_count = ENTRIES - jnp.sum(far.astype(jnp.int32))
    widen = lambda v: jnp.pad(v, (0, PAD - v.shape[0]))
    return widen(order), jnp.stack([widen(order // 8), widen(placed), widen(jnp.stack([near_count, x, q, x ^ col]))])


def on_device(start, blocks, neighbors, offsets, center, half_width):
    rows, width = start.shape
    col = lax.axis_index("col")
    x = lax.rem(lax.axis_index("slab"), X)
    q = lax.rem(lax.div(lax.axis_index("slab"), X), 4)
    order, meta = tables(neighbors, offsets, x, q, col)
    slab = lambda value, pairs: lax.ppermute(value, "slab", pairs)
    by_a = lambda value: slab(value, swaps(1))
    by_b = lambda value: slab(value, swaps(0))
    table = sorted_blocks(blocks.reshape(ENTRIES, BLOCK, BLOCK), order)

    def near_and_far(value, after):
        from_b = by_b(value)
        from_a = by_a(value)
        far = [by_a(from_b), by_b(from_a)]
        sources, _ = lax.optimization_barrier(([from_a, value, from_b], after))
        return near_terms(meta, table, sources), far

    def apply_operator(current, scale, others, first=()):
        result, seen = [], []
        for h in range(2):
            near, far = near_and_far(current[h], result or list(first))
            result.append(far_terms(meta, scale, table, far, near, [o[h] for o in others]))
            seen += [near, far]
        return result, seen

    inverse = 1.0 / half_width[0]
    once = jnp.stack([inverse, -center[0] * inverse])
    twice = jnp.stack([2.0 * inverse, -2.0 * center[0] * inverse, jnp.float32(-1.0)])

    grid = jnp.transpose(start.reshape(BLK, BLOCK, width), (0, 2, 1))
    previous = [grid[:, :WIDE], grid[:, WIDE:]]
    current, _ = apply_operator(previous, once, [previous])
    for level in range(2):
        previous, (current, _) = current, apply_operator(current, twice, [current, previous])
    by_col = lambda value, d: lax.ppermute(value, "col", [(c, c ^ d) for c in range(4)])
    device = lambda value, pairs: lax.ppermute(value, ("slab", "col"), pairs)
    aside = device(current[0], [(4 * s + c, 4 * t + (c ^ 2)) for s, t in AT_WRAP for c in range(4)])
    image, seen = apply_operator(current, once, [], [aside])
    filtered = jnp.transpose(jnp.concatenate(current, axis=1), (0, 2, 1)).reshape(rows, width)

    last = by_col(current[1], 2)
    aside, later, _ = lax.optimization_barrier((aside, current[0], seen[:2]))
    inner = [s for s in range(SLABS) if s not in dict(AT_WRAP)]
    direct = device(later, [(4 * s + c, 4 * s + (c ^ 2)) for s in inner for c in range(4)])
    back = device(aside, [(4 * t + c, 4 * s + c) for s, t in AT_WRAP for c in range(4)])
    ready, _ = lax.optimization_barrier((current + [last], seen))
    across = [direct + back, ready[2]]
    every = current + [by_col(h, 1) for h in ready[:2]] + across + [by_col(h, 1) for h in across]

    terms = outer(meta, every, image)
    moved = lambda d: device_pairs(lambda x, c: (x ^ d, c ^ x ^ d))
    parts = [lax.ppermute(terms[d], ("slab", "col"), moved(d)) for d in range(4)]
    beside_z = [slab_pairs(lambda y, z, x, d=d: (y, z ^ d, x)) for d in (1, 2, 3)]
    parts = small(scatter_kernel, [(2, PART, BLOCK)] * 4, meta, parts, "scatter")
    arrived = [slab(part, pairs) for part, pairs in zip(parts[1:], beside_z)]
    own = parts[0] + arrived[0] + (arrived[1] + arrived[2])
    own = own + slab(own, slab_pairs(lambda y, z, x: (y, z ^ 4, x)))
    own = own + slab(own, slab_pairs(lambda y, z, x: (y ^ 1, z, x)))
    own = own * (1.0 / (rows * SLABS))
    parts = [own] + [slab(own, pairs) for pairs in beside_z]
    (own,) = small(gather_kernel, [(2, BLOCK, BLOCK)], meta, parts, "gather")
    parts = [own] + [slab(own, slab_pairs(lambda y, z, x: (y, z, x ^ d))) for d in (1, 2, 3)]
    gram, projected = small(place_kernel, [(BLOCK, 4 * BLOCK)] * 2, meta, parts, "place")
    return filtered, gram, projected


def solution(mesh):
    return jax.shard_map(
        on_device,
        mesh=mesh,
        in_specs=(
            P("slab", "col"),
            P("slab", None, None, None),
            P("slab", None),
            P("slab", None),
            P(),
            P(),
        ),
        out_specs=(P("slab", "col"), P("col", None), P("col", None)),
        check_vma=False,
    )
```

```python
import functools

import jax
import jax.numpy as jnp
from jax import lax
from jax.experimental import pallas as pl
from jax.experimental.pallas import tpu as pltpu
from jax.sharding import PartitionSpec as P

BLOCK = 128
BLK = 16
WIDE = 64
ENTRIES = 128
GROUP = 16
SORTED = 16
PAD = ENTRIES + SORTED
YH, Z, X = 2, 8, 4
SLABS = YH * Z * X
AT_WRAP = [(0, 1), (31, 30), (32, 33), (63, 62)]


def slab_of(y, z, x):
    return (y * Z + z) * X + x


def swaps(first):
    pairs = []
    for s in range(first, SLABS, 2):
        t = (s + 1) % SLABS
        pairs += [(s, t), (t, s)]
    return pairs


def slab_pairs(target):
    return [(slab_of(y, z, x), slab_of(*target(y, z, x))) for y in range(YH) for z in range(Z) for x in range(X)]


def device_pairs(target):
    pairs = []
    for s in range(SLABS):
        y, z, x = s // (Z * X), s // X % Z, s % X
        for c in range(4):
            to_x, to_c = target(x, c)
            pairs.append((s * 4 + c, slab_of(y, z, to_x) * 4 + to_c))
    return pairs


def split(value):
    high = value.astype(jnp.bfloat16)
    return high, (value - high.astype(jnp.float32)).astype(jnp.bfloat16)


def across_lanes(a, b):
    return lax.dot_general(a, b, (((1,), (1,)), ((), ())), preferred_element_type=jnp.float32)


SMEM = pl.BlockSpec(memory_space=pltpu.SMEM)
VMEM = pl.BlockSpec(memory_space=pltpu.VMEM)


def sort_kernel(order, *refs):
    out = refs[-1]
    for u in range(SORTED):
        high, low = split(refs[u][0])
        out[u, :, :BLOCK] = high
        out[u, :, BLOCK:] = low


def sorted_blocks(blocks, order):
    spec = lambda u: pl.BlockSpec((1, BLOCK, BLOCK), lambda g, order: (order[g * SORTED + u], 0, 0))
    return pl.pallas_call(
        sort_kernel,
        out_shape=jax.ShapeDtypeStruct((PAD, BLOCK, 2 * BLOCK), jnp.bfloat16),
        grid_spec=pltpu.PrefetchScalarGridSpec(
            num_scalar_prefetch=1,
            grid=(PAD // SORTED,),
            in_specs=[spec(u) for u in range(SORTED)],
            out_specs=pl.BlockSpec((SORTED, BLOCK, 2 * BLOCK), lambda g, order: (g, 0, 0)),
        ),
        compiler_params=pltpu.CompilerParams(vmem_limit_bytes=16 << 20),
        cost_estimate=pl.CostEstimate(flops=0, bytes_accessed=24 << 20, transcendentals=0),
        name="sort_blocks",
    )(order, *[blocks] * SORTED)


def accumulate(meta, table, source, acc, first, last):
    def step(k, carry):
        terms, rows = [], []
        for u in range(GROUP):
            e = first + k * GROUP + u
            value = source[meta[1, e]]
            high, low = split(jnp.where(e < last, value, jnp.zeros_like(value)))
            lhs = jnp.concatenate(
                [jnp.concatenate([high, high], axis=1), jnp.concatenate([low, jnp.zeros_like(low)], axis=1)], axis=0
            )
            both = across_lanes(lhs, table[e])
            terms.append(both[:WIDE] + both[WIDE:])
            rows.append(meta[0, e])
        for u in range(GROUP):
            acc[rows[u]] += terms[u]
        return carry

    lax.fori_loop(0, lax.div(last - first + (GROUP - 1), GROUP), step, 0)


HELD = (BLK, WIDE, BLOCK)


def cost(entries):
    return pl.CostEstimate(flops=entries * 6 * BLOCK**3, bytes_accessed=entries * 4 * BLOCK**2, transcendentals=0)


def near_kernel(meta, table, *refs):
    sources, acc = refs[:3], refs[3]
    acc[...] = jnp.zeros_like(acc)
    for j in range(3):
        accumulate(meta, table, sources[j], acc, meta[2, j], meta[2, j + 1])


def near_terms(meta, table, sources):
    return pl.pallas_call(
        near_kernel,
        out_shape=jax.ShapeDtypeStruct(HELD, jnp.float32),
        in_specs=[SMEM, VMEM] + [VMEM] * 3,
        out_specs=VMEM,
        compiler_params=pltpu.CompilerParams(vmem_limit_bytes=16 << 20),
        cost_estimate=cost(80),
        name="near_terms",
    )(meta, table, *sources)


def far_kernel(parts, meta, scale, table, *refs):
    sources, near, others, out = refs[:2], refs[2], refs[3 : 3 + parts], refs[3 + parts]
    out[...] = near[...]
    for j in range(2):
        accumulate(meta, table, sources[j], out, meta[2, 3 + j], meta[2, 4 + j])
    if parts:
        value = out[...] * scale[0]
        for j in range(parts):
            value = value + others[j][...] * scale[j + 1]
        out[...] = value


def far_terms(meta, scale, table, sources, near, others):
    return pl.pallas_call(
        functools.partial(far_kernel, len(others)),
        out_shape=jax.ShapeDtypeStruct(HELD, jnp.float32),
        in_specs=[SMEM, SMEM, VMEM] + [VMEM] * (3 + len(others)),
        out_specs=VMEM,
        compiler_params=pltpu.CompilerParams(vmem_limit_bytes=16 << 20),
        cost_estimate=cost(52),
        name="far_terms",
    )(meta, scale, table, *sources, near, *others)


def outer_kernel(meta, *refs):
    every, outs, total = refs[:8], refs[10:14], refs[14]
    right = every[:2] + refs[8:10]
    total[...] = jnp.zeros_like(total)

    def step(k, carry):
        def some(ref):
            return jnp.concatenate([ref[4 * k + i] for i in range(4)], axis=-1)

        a = split(jnp.concatenate([some(ref) for ref in every], axis=0))
        b = split(jnp.concatenate([some(ref) for ref in right], axis=0))
        total[...] += across_lanes(a[0], b[0]) + (across_lanes(a[0], b[1]) + across_lanes(a[1], b[0]))
        return carry

    lax.fori_loop(0, BLK // 4, step, 0)
    for d in range(4):
        part = pl.ds(pl.multiple_of((meta[2, 6] ^ d) * BLOCK, BLOCK), BLOCK)
        for k in range(2):
            outs[d][k] = total[part, k * BLOCK : (k + 1) * BLOCK]


def outer(meta, every, image):
    return pl.pallas_call(
        outer_kernel,
        out_shape=[jax.ShapeDtypeStruct((2, BLOCK, BLOCK), jnp.float32)] * 4,
        in_specs=[SMEM] + [VMEM] * 10,
        out_specs=[VMEM] * 4,
        scratch_shapes=[pltpu.VMEM((4 * BLOCK, 2 * BLOCK), jnp.float32)],
        compiler_params=pltpu.CompilerParams(vmem_limit_bytes=12 << 20),
        cost_estimate=pl.CostEstimate(flops=6 * 2048 * 512 * 256, bytes_accessed=6 << 20, transcendentals=0),
        name="outer",
    )(meta, *every, *image)


PART = BLOCK // 4


def small(kernel, outs, meta, parts, name):
    return pl.pallas_call(
        kernel,
        out_shape=[jax.ShapeDtypeStruct(shape, jnp.float32) for shape in outs],
        in_specs=[SMEM] + [VMEM] * len(parts),
        out_specs=[VMEM] * len(outs),
        compiler_params=pltpu.CompilerParams(vmem_limit_bytes=4 << 20),
        name=name,
    )(meta, *parts)


def quarter(meta, d):
    return pl.ds(pl.multiple_of((meta[2, 7] ^ d) * PART, PART), PART)


def scatter_kernel(meta, *refs):
    for d in range(4):
        part = quarter(meta, d)
        for k in range(2):
            refs[4 + d][k] = (refs[0][k, part] + refs[1][k, part]) + (refs[2][k, part] + refs[3][k, part])


def gather_kernel(meta, *refs):
    for d in range(4):
        for k in range(2):
            refs[4][k, quarter(meta, d)] = refs[d][k]


def place_kernel(meta, *refs):
    for d in range(4):
        columns = pl.ds(pl.multiple_of((meta[2, 8] ^ d) * BLOCK, BLOCK), BLOCK)
        for k in range(2):
            refs[4 + k][:, columns] = refs[d][k]


def tables(neighbors, offsets, x, q, col):
    entry = jnp.arange(ENTRIES, dtype=jnp.int32)
    off, nbr = offsets.reshape(ENTRIES), neighbors.reshape(ENTRIES)
    by_b = ((off > 0) != ((x & 1) == 1)).astype(jnp.int32)
    kind = jnp.where(jnp.abs(off) == 2, 3 + by_b, jnp.where(off == 0, 1, 2 * by_b))
    key = kind * ENTRIES + entry
    rank = jnp.sum((key[None, :] < key[:, None]).astype(jnp.int32), axis=1)
    hit = (rank[None, :] == entry[:, None]).astype(jnp.int32)
    order = jnp.sum(hit * entry[None, :], axis=1)
    placed = jnp.sum(hit * nbr[None, :], axis=1)
    firsts = jnp.sum((kind[None, :] < jnp.arange(6)[:, None]).astype(jnp.int32), axis=1)
    widen = lambda v: jnp.pad(v, (0, PAD - v.shape[0]))
    return widen(order), jnp.stack([widen(order // 8), widen(placed), widen(jnp.concatenate([firsts, jnp.stack([x, q, x ^ col])]))])


def on_device(start, blocks, neighbors, offsets, center, half_width):
    rows, width = start.shape
    col = lax.axis_index("col")
    x = lax.rem(lax.axis_index("slab"), X)
    q = lax.rem(lax.div(lax.axis_index("slab"), X), 4)
    order, meta = tables(neighbors, offsets, x, q, col)
    slab = lambda value, pairs: lax.ppermute(value, "slab", pairs)
    by_a = lambda value: slab(value, swaps(1))
    by_b = lambda value: slab(value, swaps(0))
    table = sorted_blocks(blocks.reshape(ENTRIES, BLOCK, BLOCK), order)

    def near_and_far(value, after):
        from_b = by_b(value)
        from_a = by_a(value)
        far = [by_a(from_b), by_b(from_a)]
        sources, _ = lax.optimization_barrier(([from_a, value, from_b], after))
        return near_terms(meta, table, sources), far

    def apply_operator(current, scale, others, first=()):
        result, seen = [], []
        for h in range(2):
            near, far = near_and_far(current[h], result or list(first))
            result.append(far_terms(meta, scale, table, far, near, [o[h] for o in others]))
            seen += [near, far]
        return result, seen

    inverse = 1.0 / half_width[0]
    once = jnp.stack([inverse, -center[0] * inverse])
    twice = jnp.stack([2.0 * inverse, -2.0 * center[0] * inverse, jnp.float32(-1.0)])

    grid = jnp.transpose(start.reshape(BLK, BLOCK, width), (0, 2, 1))
    previous = [grid[:, :WIDE], grid[:, WIDE:]]
    current, _ = apply_operator(previous, once, [previous])
    for level in range(2):
        previous, (current, _) = current, apply_operator(current, twice, [current, previous])
    by_col = lambda value, d: lax.ppermute(value, "col", [(c, c ^ d) for c in range(4)])
    device = lambda value, pairs: lax.ppermute(value, ("slab", "col"), pairs)
    aside = device(current[0], [(4 * s + c, 4 * t + (c ^ 2)) for s, t in AT_WRAP for c in range(4)])
    image, seen = apply_operator(current, once, [], [aside])
    filtered = jnp.transpose(jnp.concatenate(current, axis=1), (0, 2, 1)).reshape(rows, width)

    last = by_col(current[1], 2)
    aside, later, _ = lax.optimization_barrier((aside, current[0], seen[:2]))
    inner = [s for s in range(SLABS) if s not in dict(AT_WRAP)]
    direct = device(later, [(4 * s + c, 4 * s + (c ^ 2)) for s in inner for c in range(4)])
    back = device(aside, [(4 * t + c, 4 * s + c) for s, t in AT_WRAP for c in range(4)])
    ready, _ = lax.optimization_barrier((current + [last], seen))
    across = [direct + back, ready[2]]
    every = current + [by_col(h, 1) for h in ready[:2]] + across + [by_col(h, 1) for h in across]

    terms = outer(meta, every, image)
    moved = lambda d: device_pairs(lambda x, c: (x ^ d, c ^ x ^ d))
    parts = [lax.ppermute(terms[d], ("slab", "col"), moved(d)) for d in range(4)]
    beside_z = [slab_pairs(lambda y, z, x, d=d: (y, z ^ d, x)) for d in (1, 2, 3)]
    parts = small(scatter_kernel, [(2, PART, BLOCK)] * 4, meta, parts, "scatter")
    arrived = [slab(part, pairs) for part, pairs in zip(parts[1:], beside_z)]
    own = parts[0] + arrived[0] + (arrived[1] + arrived[2])
    own = own + slab(own, slab_pairs(lambda y, z, x: (y, z ^ 4, x)))
    own = own + slab(own, slab_pairs(lambda y, z, x: (y ^ 1, z, x)))
    own = own * (1.0 / (rows * SLABS))
    parts = [own] + [slab(own, pairs) for pairs in beside_z]
    (own,) = small(gather_kernel, [(2, BLOCK, BLOCK)], meta, parts, "gather")
    parts = [own] + [slab(own, slab_pairs(lambda y, z, x: (y, z, x ^ d))) for d in (1, 2, 3)]
    gram, projected = small(place_kernel, [(BLOCK, 4 * BLOCK)] * 2, meta, parts, "place")
    return filtered, gram, projected


def solution(mesh):
    return jax.shard_map(
        on_device,
        mesh=mesh,
        in_specs=(
            P("slab", "col"),
            P("slab", None, None, None),
            P("slab", None),
            P("slab", None),
            P(),
            P(),
        ),
        out_specs=(P("slab", "col"), P("col", None), P("col", None)),
        check_vma=False,
    )
```

```python
import functools

import jax
import jax.numpy as jnp
from jax import lax
from jax.experimental import pallas as pl
from jax.experimental.pallas import tpu as pltpu
from jax.sharding import PartitionSpec as P

BLOCK = 128
BLK = 16
WIDE = 64
ENTRIES = 128
GROUP = 16
SORTED = 16
PAD = ENTRIES + SORTED
YH, Z, X = 2, 8, 4
SLABS = YH * Z * X
AT_WRAP = [(0, 1), (31, 30), (32, 33), (63, 62)]


def slab_of(y, z, x):
    return (y * Z + z) * X + x


def swaps(first):
    pairs = []
    for s in range(first, SLABS, 2):
        t = (s + 1) % SLABS
        pairs += [(s, t), (t, s)]
    return pairs


def slab_pairs(target):
    return [(slab_of(y, z, x), slab_of(*target(y, z, x))) for y in range(YH) for z in range(Z) for x in range(X)]


def device_pairs(target):
    pairs = []
    for s in range(SLABS):
        y, z, x = s // (Z * X), s // X % Z, s % X
        for c in range(4):
            to_x, to_c = target(x, c)
            pairs.append((s * 4 + c, slab_of(y, z, to_x) * 4 + to_c))
    return pairs


def split(value):
    high = value.astype(jnp.bfloat16)
    return high, (value - high.astype(jnp.float32)).astype(jnp.bfloat16)


def across_lanes(a, b):
    return lax.dot_general(a, b, (((1,), (1,)), ((), ())), preferred_element_type=jnp.float32)


SMEM = pl.BlockSpec(memory_space=pltpu.SMEM)
VMEM = pl.BlockSpec(memory_space=pltpu.VMEM)


def sort_kernel(order, *refs):
    out = refs[-1]
    for u in range(SORTED):
        high, low = split(refs[u][0])
        out[u, :, :BLOCK] = high
        out[u, :, BLOCK:] = low


def sorted_blocks(blocks, order):
    spec = lambda u: pl.BlockSpec((1, BLOCK, BLOCK), lambda g, order: (order[g * SORTED + u], 0, 0))
    return pl.pallas_call(
        sort_kernel,
        out_shape=jax.ShapeDtypeStruct((PAD, BLOCK, 2 * BLOCK), jnp.bfloat16),
        grid_spec=pltpu.PrefetchScalarGridSpec(
            num_scalar_prefetch=1,
            grid=(PAD // SORTED,),
            in_specs=[spec(u) for u in range(SORTED)],
            out_specs=pl.BlockSpec((SORTED, BLOCK, 2 * BLOCK), lambda g, order: (g, 0, 0)),
        ),
        compiler_params=pltpu.CompilerParams(vmem_limit_bytes=16 << 20),
        cost_estimate=pl.CostEstimate(flops=0, bytes_accessed=24 << 20, transcendentals=0),
        name="sort_blocks",
    )(order, *[blocks] * SORTED)


def accumulate(meta, table, source, acc, first, last):
    def step(k, carry):
        terms, rows = [], []
        for u in range(GROUP):
            e = first + k * GROUP + u
            value = source[meta[1, e]]
            high, low = split(jnp.where(e < last, value, jnp.zeros_like(value)))
            lhs = jnp.concatenate(
                [jnp.concatenate([high, high], axis=1), jnp.concatenate([low, jnp.zeros_like(low)], axis=1)], axis=0
            )
            both = across_lanes(lhs, table[e])
            terms.append(both[:WIDE] + both[WIDE:])
            rows.append(meta[0, e])
        for u in range(GROUP):
            acc[rows[u]] += terms[u]
        return carry

    lax.fori_loop(0, lax.div(last - first + (GROUP - 1), GROUP), step, 0)


HELD = (BLK, WIDE, BLOCK)


def cost(entries):
    return pl.CostEstimate(flops=entries * 6 * BLOCK**3, bytes_accessed=entries * 4 * BLOCK**2, transcendentals=0)


def near_kernel(meta, table, *refs):
    sources, acc = refs[:3], refs[3]
    acc[...] = jnp.zeros_like(acc)
    for j in range(3):
        accumulate(meta, table, sources[j], acc, meta[2, j], meta[2, j + 1])


def near_terms(meta, table, sources):
    return pl.pallas_call(
        near_kernel,
        out_shape=jax.ShapeDtypeStruct(HELD, jnp.float32),
        in_specs=[SMEM, VMEM] + [VMEM] * 3,
        out_specs=VMEM,
        compiler_params=pltpu.CompilerParams(vmem_limit_bytes=16 << 20),
        cost_estimate=cost(80),
        name="near_terms",
    )(meta, table, *sources)


def far_kernel(parts, meta, scale, table, *refs):
    sources, near, others, out = refs[:2], refs[2], refs[3 : 3 + parts], refs[3 + parts]
    out[...] = near[...]
    for j in range(2):
        accumulate(meta, table, sources[j], out, meta[2, 3 + j], meta[2, 4 + j])
    if parts:
        value = out[...] * scale[0]
        for j in range(parts):
            value = value + others[j][...] * scale[j + 1]
        out[...] = value


def far_terms(meta, scale, table, sources, near, others):
    return pl.pallas_call(
        functools.partial(far_kernel, len(others)),
        out_shape=jax.ShapeDtypeStruct(HELD, jnp.float32),
        in_specs=[SMEM, SMEM, VMEM] + [VMEM] * (3 + len(others)),
        out_specs=VMEM,
        compiler_params=pltpu.CompilerParams(vmem_limit_bytes=16 << 20),
        cost_estimate=cost(52),
        name="far_terms",
    )(meta, scale, table, *sources, near, *others)


def outer_kernel(meta, *refs):
    every, outs, total = refs[:8], refs[10:14], refs[14]
    right = every[:2] + refs[8:10]
    total[...] = jnp.zeros_like(total)

    def step(k, carry):
        def some(ref):
            return jnp.concatenate([ref[4 * k + i] for i in range(4)], axis=-1)

        a = split(jnp.concatenate([some(ref) for ref in every], axis=0))
        b = split(jnp.concatenate([some(ref) for ref in right], axis=0))
        total[...] += across_lanes(a[0], b[0]) + (across_lanes(a[0], b[1]) + across_lanes(a[1], b[0]))
        return carry

    lax.fori_loop(0, BLK // 4, step, 0)
    for d in range(4):
        part = pl.ds(pl.multiple_of((meta[2, 6] ^ d) * BLOCK, BLOCK), BLOCK)
        for k in range(2):
            outs[d][k] = total[part, k * BLOCK : (k + 1) * BLOCK]


def outer(meta, every, image):
    return pl.pallas_call(
        outer_kernel,
        out_shape=[jax.ShapeDtypeStruct((2, BLOCK, BLOCK), jnp.float32)] * 4,
        in_specs=[SMEM] + [VMEM] * 10,
        out_specs=[VMEM] * 4,
        scratch_shapes=[pltpu.VMEM((4 * BLOCK, 2 * BLOCK), jnp.float32)],
        compiler_params=pltpu.CompilerParams(vmem_limit_bytes=12 << 20),
        cost_estimate=pl.CostEstimate(flops=6 * 2048 * 512 * 256, bytes_accessed=6 << 20, transcendentals=0),
        name="outer",
    )(meta, *every, *image)


PART = BLOCK // 4


def small(kernel, outs, meta, parts, name):
    return pl.pallas_call(
        kernel,
        out_shape=[jax.ShapeDtypeStruct(shape, jnp.float32) for shape in outs],
        in_specs=[SMEM] + [VMEM] * len(parts),
        out_specs=[VMEM] * len(outs),
        compiler_params=pltpu.CompilerParams(vmem_limit_bytes=4 << 20),
        name=name,
    )(meta, *parts)


def quarter(meta, d):
    return pl.ds(pl.multiple_of((meta[2, 7] ^ d) * PART, PART), PART)


def scatter_kernel(meta, *refs):
    for d in range(4):
        part = quarter(meta, d)
        for k in range(2):
            refs[4 + d][k] = (refs[0][k, part] + refs[1][k, part]) + (refs[2][k, part] + refs[3][k, part])


def gather_kernel(meta, *refs):
    for d in range(4):
        for k in range(2):
            refs[4][k, quarter(meta, d)] = refs[d][k]


def place_kernel(meta, *refs):
    for d in range(4):
        columns = pl.ds(pl.multiple_of((meta[2, 8] ^ d) * BLOCK, BLOCK), BLOCK)
        for k in range(2):
            refs[4 + k][:, columns] = refs[d][k]


def tables(neighbors, offsets, x, q, col):
    entry = jnp.arange(ENTRIES, dtype=jnp.int32)
    off, nbr = offsets.reshape(ENTRIES), neighbors.reshape(ENTRIES)
    by_b = ((off > 0) != ((x & 1) == 1)).astype(jnp.int32)
    kind = jnp.where(jnp.abs(off) == 2, 3 + by_b, jnp.where(off == 0, 1, 2 * by_b))
    key = kind * ENTRIES + entry
    rank = jnp.sum((key[None, :] < key[:, None]).astype(jnp.int32), axis=1)
    hit = (rank[None, :] == entry[:, None]).astype(jnp.int32)
    order = jnp.sum(hit * entry[None, :], axis=1)
    placed = jnp.sum(hit * nbr[None, :], axis=1)
    firsts = jnp.sum((kind[None, :] < jnp.arange(6)[:, None]).astype(jnp.int32), axis=1)
    widen = lambda v: jnp.pad(v, (0, PAD - v.shape[0]))
    return widen(order), jnp.stack([widen(order // 8), widen(placed), widen(jnp.concatenate([firsts, jnp.stack([x, q, x ^ col])]))])


def on_device(start, blocks, neighbors, offsets, center, half_width):
    rows, width = start.shape
    col = lax.axis_index("col")
    x = lax.rem(lax.axis_index("slab"), X)
    q = lax.rem(lax.div(lax.axis_index("slab"), X), 4)
    order, meta = tables(neighbors, offsets, x, q, col)
    slab = lambda value, pairs: lax.ppermute(value, "slab", pairs)
    by_a = lambda value: slab(value, swaps(1))
    by_b = lambda value: slab(value, swaps(0))
    table = sorted_blocks(blocks.reshape(ENTRIES, BLOCK, BLOCK), order)

    def near_and_far(value, after):
        from_b = by_b(value)
        from_a = by_a(value)
        far = [by_a(from_b), by_b(from_a)]
        sources, _ = lax.optimization_barrier(([from_a, value, from_b], after))
        return near_terms(meta, table, sources), far

    def apply_operator(current, scale, others, first=()):
        result, seen = [], []
        for h in range(2):
            near, far = near_and_far(current[h], result or list(first))
            result.append(far_terms(meta, scale, table, far, near, [o[h] for o in others]))
            seen += [near, far]
        return result, seen

    inverse = 1.0 / half_width[0]
    once = jnp.stack([inverse, -center[0] * inverse])
    twice = jnp.stack([2.0 * inverse, -2.0 * center[0] * inverse, jnp.float32(-1.0)])

    grid = jnp.transpose(start.reshape(BLK, BLOCK, width), (0, 2, 1))
    previous = [grid[:, :WIDE], grid[:, WIDE:]]
    current, _ = apply_operator(previous, once, [previous])
    for level in range(2):
        previous, (current, _) = current, apply_operator(current, twice, [current, previous])
    by_col = lambda value, d: lax.ppermute(value, "col", [(c, c ^ d) for c in range(4)])
    device = lambda value, pairs: lax.ppermute(value, ("slab", "col"), pairs)
    aside = device(current[0], [(4 * s + c, 4 * t + (c ^ 2)) for s, t in AT_WRAP for c in range(4)])
    image, seen = apply_operator(current, once, [], [aside])
    filtered = jnp.transpose(jnp.concatenate(current, axis=1), (0, 2, 1)).reshape(rows, width)

    last = by_col(current[1], 2)
    aside, later, _ = lax.optimization_barrier((aside, current[0], seen[:2]))
    inner = [s for s in range(SLABS) if s not in dict(AT_WRAP)]
    direct = device(later, [(4 * s + c, 4 * s + (c ^ 2)) for s in inner for c in range(4)])
    back = device(aside, [(4 * t + c, 4 * s + c) for s, t in AT_WRAP for c in range(4)])
    ready, _ = lax.optimization_barrier((current, seen))
    last, _ = lax.optimization_barrier((last, image))
    across = [direct + back, last]
    every = current + [by_col(h, 1) for h in ready] + across + [by_col(h, 1) for h in across]

    terms = outer(meta, every, image)
    moved = lambda d: device_pairs(lambda x, c: (x ^ d, c ^ x ^ d))
    parts = [lax.ppermute(terms[d], ("slab", "col"), moved(d)) for d in range(4)]
    beside_z = [slab_pairs(lambda y, z, x, d=d: (y, z ^ d, x)) for d in (1, 2, 3)]
    parts = small(scatter_kernel, [(2, PART, BLOCK)] * 4, meta, parts, "scatter")
    arrived = [slab(part, pairs) for part, pairs in zip(parts[1:], beside_z)]
    own = parts[0] + arrived[0] + (arrived[1] + arrived[2])
    own = own + slab(own, slab_pairs(lambda y, z, x: (y, z ^ 4, x)))
    own = own + slab(own, slab_pairs(lambda y, z, x: (y ^ 1, z, x)))
    own = own * (1.0 / (rows * SLABS))
    parts = [own] + [slab(own, pairs) for pairs in beside_z]
    (own,) = small(gather_kernel, [(2, BLOCK, BLOCK)], meta, parts, "gather")
    parts = [own] + [slab(own, slab_pairs(lambda y, z, x: (y, z, x ^ d))) for d in (1, 2, 3)]
    gram, projected = small(place_kernel, [(BLOCK, 4 * BLOCK)] * 2, meta, parts, "place")
    return filtered, gram, projected


def solution(mesh):
    return jax.shard_map(
        on_device,
        mesh=mesh,
        in_specs=(
            P("slab", "col"),
            P("slab", None, None, None),
            P("slab", None),
            P("slab", None),
            P(),
            P(),
        ),
        out_specs=(P("slab", "col"), P("col", None), P("col", None)),
        check_vma=False,
    )
```
